32 devices in a mesh: groups: 2 (over y), pair: 4 (over z), amp: 2 (over x), rep: 2 (over core).
Axes of the slice: x: 2, y: 2, z: 4, core: 2. Of those that a mesh axis runs over, the one named last changes fastest.
Arguments:
- amplitudes: float32 [4, 1728, 768], P('groups', 'pair', 'amp'), parts along dimension 0, may hold values from -8 to 8
- integrals: float32 [4, 1728, 2048], P('groups', 'pair', 'rep'), parts along dimension 0, may hold values from -0.21875 to 0.21875
- tile_map: int32 [4, 108], P('groups'), parts along dimension 0, may hold values from 0 to 107, as said below
- residual: float32 [2, 1024, 4, 768], P('rep', 'pair', 'groups', 'amp'), parts along dimension 2, may hold values from -8 to 8
Outputs:
- ladder: float32 [2, 1024, 4, 768], P('rep', 'pair', 'groups', 'amp'), parts along dimension 2
The draws below stay inside these ranges and needn't reach their ends.
There are 2 independent parts, one for each index of `groups`. The reference program is written for one: setup_inputs(seed, part) draws one part's arguments, and reference() takes and returns one part's arrays. A program takes and returns all parts, laid end to end along the dimension named above; each array names one. Nothing has to cross between parts.
Inputs may be any that keep to these rules, and one draw needn't show every extreme that they name: For each irrep, tile_map names every block 0 to 107 exactly once. Split the entries into runs of 27 (the blocks stored on one index of pair) and the block numbers into ranges of 27: each run takes between 6 and 7 blocks from each range, and 7 from some range.
All inputs are finite; a program needn't handle non-finite values.
Results may differ from the reference program's by a relative error of at most 0.0001.
Values sent between devices are 32-bit elements; how exact they have to be, the bound alone decides.
A program may use at most 64 MiB of HBM per device.

```python
import jax
import jax.numpy as jnp
from jax import lax

TILE = 16
TD = 27
WH = 1024
NT = 108
P_SIZE = 1728
O = 768
W = 2048
N_PAIR = 4
N_REP = 2


def row_permutations(key, count, length):

    def single(sub_key):
        return jax.random.permutation(sub_key, length)
    return jax.vmap(single)(jax.random.split(key, count))


def draw_tile_map(key, part):
    key = jax.random.fold_in(key, 7)
    layouts = []
    for irrep in range(2):
        sub_key = jax.random.fold_in(key, irrep)
        home_perm = jax.random.permutation(jax.random.fold_in(sub_key, 1), N_PAIR)
        shift_perm = jax.random.permutation(jax.random.fold_in(sub_key, 2), N_PAIR)
        slot_perm = row_permutations(jax.random.fold_in(sub_key, 3), N_PAIR, TD)
        local_perm = row_permutations(jax.random.fold_in(sub_key, 4), N_PAIR, TD)
        devices = jnp.arange(N_PAIR, dtype=jnp.int32)[:, None]
        counter = jnp.arange(TD, dtype=jnp.int32)[None, :]
        home_of = home_perm[(shift_perm[devices] + counter) % N_PAIR]
        local_tile = local_perm[home_of, jnp.broadcast_to(counter, home_of.shape)]
        tile_ids = home_of * TD + local_tile
        placed = jnp.zeros((N_PAIR, TD), jnp.int32).at[jnp.broadcast_to(devices, slot_perm.shape), slot_perm].set(tile_ids.astype(jnp.int32))
        layouts.append(placed.reshape(N_PAIR * TD))
    return jnp.stack(layouts).astype(jnp.int32)


def raised(drawn, own_key, source, target, parts, factor):
    owner, partner = [(jnp.arange(drawn.shape[axis_at]) // (drawn.shape[axis_at] // parts)).reshape([-1 if axis == axis_at else 1 for axis in range(drawn.ndim)]) for axis_at in (source, target)]
    chosen = jax.random.permutation(own_key, parts)[partner]
    strong = (owner == chosen) | (owner == (partner + parts // 2) % parts)
    return jnp.where(strong, factor * drawn, drawn)


def steps_of(rng, shape, pieces, least, high):
    loudness, own = 1.0, jax.random.fold_in(rng, 6)
    for dim, parts in pieces:
        draws = jnp.exp(jax.random.uniform(jax.random.fold_in(own, dim), (parts,), jnp.float32, least / len(pieces), high / len(pieces)))
        loudness = loudness * jnp.repeat(draws, shape[dim] // parts).reshape([-1 if axis == dim else 1 for axis in range(len(shape))])
    return loudness


def bell_draw(own_key, extent, deviation, most, cuts=(), held_as=jnp.bfloat16):
    result = deviation * jax.random.normal(own_key, extent, jnp.float32)
    if cuts:
        result = result * steps_of(own_key, extent, cuts, -0.22, 0.18)
    return jnp.clip(result, -most, most).astype(held_as)


def heavy_noise(key, dims, scale, bound, shards, heavy, kind=jnp.bfloat16):
    entries = scale * jax.random.normal(key, dims, jnp.float32)
    if shards:
        entries = entries * steps_of(key, dims, shards, -0.22, 0.18)
    return jnp.clip(raised(entries, jax.random.fold_in(key, 3), *heavy), -bound, bound).astype(kind)


def setup_inputs(seed: int = 0, part: int = 0) -> dict:
    key_of = jax.random.split(jax.random.key(seed), 5)
    part_keys = jax.random.split(jax.random.fold_in(key_of[4], part), 5)
    amplitudes = bell_draw(part_keys[0], (2, P_SIZE, O), 1.0, 8.0, ((1, 4), (2, 2)), jnp.float32)
    integrals = heavy_noise(part_keys[1], (2, P_SIZE, W), P_SIZE ** -0.5, 0.21875, ((1, 4), (2, 2)), (1, 2, 4, 2.0), jnp.float32)
    tile_map = draw_tile_map(jax.random.fold_in(jax.random.fold_in(key_of[4], part), 71), part)
    residual = bell_draw(part_keys[3], (N_REP, WH, 2, O), 1.0, 8.0, ((0, 2), (1, 4), (3, 2)), jnp.float32)
    return dict(amplitudes=amplitudes, integrals=integrals, tile_map=tile_map, residual=residual)


def reference(amplitudes, integrals, tile_map, residual):
    totals = []
    for irrep in range(2):
        blocks = amplitudes[irrep].reshape(NT, TILE, O)
        picked = jnp.take(blocks, tile_map[irrep].astype(jnp.int32), axis=0).reshape(NT * TILE, O)
        product = lax.dot_general(integrals[irrep], picked, (((0,), (0,)), ((), ())), precision=lax.Precision.HIGHEST, preferred_element_type=jnp.float32)
        totals.append(product)
    ladder_sum = jnp.stack(totals, axis=1)
    return residual + 0.5 * ladder_sum.reshape(N_REP, WH, 2, O)
```

```python
import functools

import jax
import jax.numpy as jnp
from jax import lax
from jax.experimental import pallas as pl
from jax.experimental.pallas import tpu as pltpu
from jax.sharding import PartitionSpec as P

TILE = 16
HALF = TILE // 2
BLOCKS = 4
MESH = pl.DeviceIdType.MESH


def table_kernel(n, most, map_ref, send_ref, pick_ref, count_ref):
    me = lax.axis_index("pair")
    slots = map_ref.shape[1] // n
    scale = ((1 << 20) + slots - 1) // slots
    low = me * slots

    for g in range(2):

        @pl.loop(0, n)
        def _(d):
            for j in range(most + 1):
                send_ref[g, d * (most + 1) + j] = 0
            found = jnp.int32(0)
            for k in range(slots):
                tile = map_ref[g, d * slots + k]
                mine = (tile >= low) & (tile < low + slots)
                send_ref[g, d * (most + 1) + found] = jnp.where(mine, tile - low, 0)
                found = found + mine.astype(jnp.int32)
            count_ref[d] = 0

        for k in range(slots):
            tile = map_ref[g, low + k]
            home = lax.shift_right_logical(tile * scale, 20)
            rank = count_ref[home]
            pick_ref[g, k] = home * most + rank
            count_ref[home] = rank + 1


def split(x):
    high = x.astype(jnp.bfloat16)
    return high, (x - high.astype(jnp.float32)).astype(jnp.bfloat16)


def ladder_kernel(
    n,
    most,
    send_tab,
    pick_tab,
    amps,
    ints_hbm,
    out,
    ints,
    packed,
    pool0,
    pool1,
    ints_hi,
    ints_lo,
    amp_hi,
    amp_lo,
    part,
    from_left,
    from_right,
    load_sem,
    a_send,
    a_recv,
    s_send,
    s_recv,
    r_send,
    r_recv,
    l_send,
    l_recv,
):
    me = lax.axis_index("pair")
    core = lax.axis_index("rep")
    slots = amps.shape[1]
    rows = part.shape[1]
    block = rows // BLOCKS
    chunk = rows // n
    per_block = n // BLOCKS
    pools = (pool0, pool1)

    loads = [pltpu.make_async_copy(ints_hbm.at[g], ints.at[g], load_sem.at[g]) for g in range(2)]
    for load in loads:
        load.start()

    barrier = pltpu.get_barrier_semaphore()

    @pl.loop(1, n)
    def _(off):
        pl.semaphore_signal(
            barrier, inc=1, device_id={"pair": lax.rem(me + off, n)}, device_id_type=MESH
        )

    pl.semaphore_signal(barrier, inc=1, device_id={"rep": 1 - core}, device_id_type=MESH)

    def pack(g):
        @pl.loop(1, n)
        def _(off):
            d = lax.rem(me + off, n)
            for j in range(most):
                packed[g, off, j] = amps[g, send_tab[g, d * (most + 1) + j], core]

    def exchange(g, off):
        source = lax.rem(me - off + n, n)
        target = lax.rem(me + off, n)
        return (
            pltpu.make_async_remote_copy(
                src_ref=packed.at[g, off],
                dst_ref=pools[g].at[core, pl.ds(me * most, most)],
                send_sem=a_send.at[g, off],
                recv_sem=a_recv.at[g, off],
                device_id={"pair": target},
                device_id_type=MESH,
            ),
            pltpu.make_async_remote_copy(
                src_ref=pools[g].at[core, pl.ds(source * most, most)],
                dst_ref=pools[g].at[core, pl.ds(source * most, most)],
                send_sem=s_send.at[g, off],
                recv_sem=s_recv.at[g, off],
                device_id={"rep": 1 - core},
                device_id_type=MESH,
            ),
        )

    pack(0)
    pl.semaphore_wait(barrier, n)
    for g in range(2):
        if g == 1:
            pack(1)

        @pl.loop(1, n)
        def _(off):
            exchange(g, off)[0].start()

    for g in range(2):
        for j in range(most):
            for h in range(2):
                pools[g][h, me * most + j] = amps[g, send_tab[g, me * (most + 1) + j], h]

    for g in range(2):
        loads[g].wait()

        @pl.loop(0, BLOCKS)
        def _(b):
            columns = pl.ds(pl.multiple_of(b * block, block), block)
            high, low = split(ints[g, :, columns].T)
            ints_hi[g, columns, :] = high
            ints_lo[g, columns, :] = low

    def send_right(g, t, src):
        return pltpu.make_async_remote_copy(
            src_ref=src,
            dst_ref=from_left.at[g, t],
            send_sem=r_send.at[g, t],
            recv_sem=r_recv.at[g, t],
            device_id={"pair": lax.rem(me + 1, n)},
            device_id_type=MESH,
        )

    def send_left(g, t, src):
        return pltpu.make_async_remote_copy(
            src_ref=src,
            dst_ref=from_right.at[g, t],
            send_sem=l_send.at[g, t],
            recv_sem=l_recv.at[g, t],
            device_id={"pair": lax.rem(me - 1 + n, n)},
            device_id_type=MESH,
        )

    def own(t):
        return pl.ds(pl.multiple_of(t * chunk, chunk), chunk)

    for g in range(2):

        @pl.loop(1, n)
        def _(off):
            arrive, pass_on = exchange(g, off)
            arrive.wait_recv()
            pass_on.start()

        @pl.loop(1, n)
        def _(off):
            exchange(g, off)[1].wait_recv()

        @pl.loop(0, slots)
        def _(k):
            where = pick_tab[g, k]
            tile = jnp.concatenate([pools[g][0, where], pools[g][1, where]], axis=0)
            high, low = split(tile)
            at = pl.ds(pl.multiple_of(k * TILE, TILE), TILE)
            amp_hi[g, at, :] = high
            amp_lo[g, at, :] = low

        @pl.loop(0, BLOCKS)
        def _(i):
            b = jnp.where(me < n // 2, BLOCKS - 1 - i, i)
            at = pl.ds(pl.multiple_of(b * block, block), block)
            dot = functools.partial(jnp.dot, preferred_element_type=jnp.float32)
            part[g, at, :] = (
                dot(ints_hi[g, at, :], amp_lo[g])
                + dot(ints_lo[g, at, :], amp_hi[g])
                + dot(ints_hi[g, at, :], amp_hi[g])
            )

            @pl.loop(0, per_block)
            def _(j):
                t = b * per_block + jnp.where(me < n // 2, per_block - 1 - j, j)

                @pl.when((me == 0) & (t > 0))
                def _():
                    send_right(g, t, part.at[g, own(t)]).start()

                @pl.when((me == n - 1) & (t < n - 1))
                def _():
                    send_left(g, t, part.at[g, own(t)]).start()

    def forward_right(g, t):
        @pl.when((t > me) & (me > 0))
        def _():
            copy = send_right(g, t, from_left.at[g, t])
            copy.wait_recv()
            from_left[g, t] = from_left[g, t] + part[g, own(t), :]
            copy.start()

    def forward_left(g, t):
        @pl.when((t < me) & (me < n - 1))
        def _():
            copy = send_left(g, t, from_right.at[g, t])
            copy.wait_recv()
            from_right[g, t] = from_right[g, t] + part[g, own(t), :]
            copy.start()

    for g in range(2):

        @pl.loop(0, n)
        def _(i):
            @pl.when(me < n // 2)
            def _():
                forward_right(g, n - 1 - i)
                forward_left(g, i)

            @pl.when(me >= n // 2)
            def _():
                forward_left(g, i)
                forward_right(g, n - 1 - i)

    for g in range(2):
        out[g] = part[g, own(me), :]

        @pl.when(me > 0)
        def _():
            send_right(g, me, from_left.at[g, me]).wait_recv()
            out[g] = out[g] + from_left[g, me]

        @pl.when(me < n - 1)
        def _():
            send_left(g, me, from_right.at[g, me]).wait_recv()
            out[g] = out[g] + from_right[g, me]

    for g in range(2):

        @pl.loop(1, n)
        def _(off):
            arrive, pass_on = exchange(g, off)
            arrive.wait_send()
            pass_on.wait_send()

        @pl.loop(0, n)
        def _(t):
            @pl.when(t > me)
            def _():
                send_right(g, t, from_left.at[g, t]).wait_send()

            @pl.when(t < me)
            def _():
                send_left(g, t, from_right.at[g, t]).wait_send()


def local(n, amplitudes, integrals, tile_map, residual):
    depth, occ = amplitudes.shape[1:]
    rows = integrals.shape[2]
    slots = depth // TILE
    most = (slots + n - 1) // n
    chunk = rows // n
    smem = pl.BlockSpec(memory_space=pltpu.SMEM)
    vmem = pl.BlockSpec(memory_space=pltpu.VMEM)
    send_tab, pick_tab = pl.pallas_call(
        functools.partial(table_kernel, n, most),
        out_shape=(
            jax.ShapeDtypeStruct((2, n * (most + 1)), jnp.int32),
            jax.ShapeDtypeStruct((2, slots), jnp.int32),
        ),
        in_specs=[smem],
        out_specs=(smem, smem),
        scratch_shapes=[pltpu.SMEM((n,), jnp.int32)],
    )(tile_map)
    f32, bf16 = jnp.float32, jnp.bfloat16
    dma = pltpu.SemaphoreType.DMA
    flops = 2 * 3 * 2 * depth * rows * occ
    summed = pl.pallas_call(
        functools.partial(ladder_kernel, n, most),
        out_shape=jax.ShapeDtypeStruct((2, chunk, occ), f32),
        in_specs=[smem, smem, vmem, pl.BlockSpec(memory_space=pl.ANY)],
        out_specs=vmem,
        scratch_shapes=[
            pltpu.VMEM((2, depth, rows), f32),
            pltpu.VMEM((2, n, most, HALF, occ), f32),
            pltpu.VMEM((2, n * most, HALF, occ), f32),
            pltpu.VMEM((2, n * most, HALF, occ), f32),
            pltpu.VMEM((2, rows, depth), bf16),
            pltpu.VMEM((2, rows, depth), bf16),
            pltpu.VMEM((2, depth, occ), bf16),
            pltpu.VMEM((2, depth, occ), bf16),
            pltpu.VMEM((2, rows, occ), f32),
            pltpu.VMEM((2, n, chunk, occ), f32),
            pltpu.VMEM((2, n, chunk, occ), f32),
            dma((2,)),
        ]
        + [dma((2, n))] * 8,
        compiler_params=pltpu.CompilerParams(
            collective_id=0, has_side_effects=True, vmem_limit_bytes=56 * 1024 * 1024
        ),
        cost_estimate=pl.CostEstimate(
            flops=flops, bytes_accessed=4 * (integrals.size + amplitudes.size), transcendentals=0
        ),
    )(
        send_tab,
        pick_tab,
        amplitudes.reshape(2, slots, 2, HALF, occ),
        integrals,
    )
    return residual + 0.5 * jnp.transpose(summed, (1, 0, 2))[None]


def solution(mesh):
    placed = (
        P("groups", "pair", "amp"),
        P("groups", "pair", "rep"),
        P("groups", None),
        P("rep", "pair", "groups", "amp"),
    )
    return jax.shard_map(
        functools.partial(local, mesh.shape["pair"]),
        mesh=mesh,
        in_specs=placed,
        out_specs=P("rep", "pair", "groups", "amp"),
        check_vma=False,
    )
```

```python
import functools

import jax
import jax.numpy as jnp
from jax import lax
from jax.experimental import pallas as pl
from jax.experimental.pallas import tpu as pltpu
from jax.sharding import PartitionSpec as P

TILE = 16
HALF = TILE // 2
BLOCKS = 4
MESH = pl.DeviceIdType.MESH


def table_kernel(n, most, map_ref, send_ref, pick_ref, count_ref):
    me = lax.axis_index("pair")
    slots = map_ref.shape[1] // n
    scale = ((1 << 20) + slots - 1) // slots
    low = me * slots

    for g in range(2):

        @pl.loop(0, n)
        def _(d):
            for j in range(most + 1):
                send_ref[g, d * (most + 1) + j] = 0
            found = jnp.int32(0)
            for k in range(slots):
                tile = map_ref[g, d * slots + k]
                mine = (tile >= low) & (tile < low + slots)
                send_ref[g, d * (most + 1) + found] = jnp.where(mine, tile - low, 0)
                found = found + mine.astype(jnp.int32)

        runs = [(g, me)] if g == 0 else [(1, me), (2, jnp.where(me < n // 2, 0, n - 1))]
        for row, run in runs:

            @pl.loop(0, n)
            def _(d):
                count_ref[d] = 0

            for k in range(slots):
                tile = map_ref[g, run * slots + k]
                home = lax.shift_right_logical(tile * scale, 20)
                rank = count_ref[home]
                pick_ref[row, k] = home * most + rank
                count_ref[home] = rank + 1


def split(x):
    high = x.astype(jnp.bfloat16)
    return high, (x - high.astype(jnp.float32)).astype(jnp.bfloat16)


def ladder_kernel(
    n,
    most,
    proxy,
    send_tab,
    pick_tab,
    amps,
    ints_hbm,
    out,
    ints,
    packed,
    pool0,
    pool1,
    ints_hi,
    ints_lo,
    amp_hi,
    amp_lo,
    part,
    from_left,
    from_right,
    pool_end,
    end_ints,
    end_hi,
    end_lo,
    end_amp_hi,
    end_amp_lo,
    load_sem,
    a_send,
    a_recv,
    s_send,
    s_recv,
    r_send,
    r_recv,
    l_send,
    l_recv,
    p_send,
    p_recv,
    q_send,
    q_recv,
    i_send,
    i_recv,
    x_send,
    x_recv,
    f_sem,
):
    me = lax.axis_index("pair")
    core = lax.axis_index("rep")
    column = lax.axis_index("amp")
    end = jnp.where(me < n // 2, 0, n - 1)
    at_end = me == end
    helper = jnp.clip(end, 1, n - 2)
    is_helper = me == helper
    first_right = (0, 1 if proxy else 0)
    first_left = (n - 1, n - 2 if proxy else n - 1)
    slots = amps.shape[1]
    rows = part.shape[1]
    block = rows // BLOCKS
    chunk = rows // n
    per_block = n // BLOCKS
    pools = (pool0, pool1)

    loads = [pltpu.make_async_copy(ints_hbm.at[g], ints.at[g], load_sem.at[g]) for g in range(2)]
    for load in loads:
        load.start()

    barrier = pltpu.get_barrier_semaphore()

    @pl.loop(1, n)
    def _(off):
        pl.semaphore_signal(
            barrier, inc=1, device_id={"pair": lax.rem(me + off, n)}, device_id_type=MESH
        )

    pl.semaphore_signal(barrier, inc=1, device_id={"rep": 1 - core}, device_id_type=MESH)
    if proxy:
        pl.semaphore_signal(barrier, inc=1, device_id={"amp": 1 - column}, device_id_type=MESH)

    def pack(g):
        @pl.loop(0 if proxy and g == 1 else 1, n)
        def _(off):
            d = lax.rem(me + off, n)
            for j in range(most):
                packed[g, off, j] = amps[g, send_tab[g, d * (most + 1) + j], core]

    def exchange(g, off):
        source = lax.rem(me - off + n, n)
        target = lax.rem(me + off, n)
        return (
            pltpu.make_async_remote_copy(
                src_ref=packed.at[g, off],
                dst_ref=pools[g].at[core, pl.ds(me * most, most)],
                send_sem=a_send.at[g, off],
                recv_sem=a_recv.at[g, off],
                device_id={"pair": target},
                device_id_type=MESH,
            ),
            pltpu.make_async_remote_copy(
                src_ref=pools[g].at[core, pl.ds(source * most, most)],
                dst_ref=pools[g].at[core, pl.ds(source * most, most)],
                send_sem=s_send.at[g, off],
                recv_sem=s_recv.at[g, off],
                device_id={"rep": 1 - core},
                device_id_type=MESH,
            ),
        )

    def to_helper(off, d):
        return pltpu.make_async_remote_copy(
            src_ref=packed.at[1, off],
            dst_ref=pool_end.at[core, pl.ds(me * most, most)],
            send_sem=a_send.at[1, off],
            recv_sem=p_recv.at[me],
            device_id={"pair": jnp.clip(d, 1, n - 2)},
            device_id_type=MESH,
        )

    def end_pass(home):
        rows_at = (core, pl.ds(home * most, most))
        return pltpu.make_async_remote_copy(
            src_ref=pool_end.at[rows_at],
            dst_ref=pool_end.at[rows_at],
            send_sem=q_send.at[home],
            recv_sem=q_recv.at[home],
            device_id={"rep": 1 - core},
            device_id_type=MESH,
        )

    others = (core, pl.ds(jnp.where(end == 0, most, 0), (n - 1) * most))

    def to_end():
        return pltpu.make_async_remote_copy(
            src_ref=pool_end.at[others],
            dst_ref=pool1.at[others],
            send_sem=f_sem.at[0],
            recv_sem=f_sem.at[1],
            device_id={"pair": end},
            device_id_type=MESH,
        )

    def end_share():
        return pltpu.make_async_remote_copy(
            src_ref=pool1.at[others],
            dst_ref=pool1.at[others],
            send_sem=f_sem.at[2],
            recv_sem=f_sem.at[3],
            device_id={"rep": 1 - core},
            device_id_type=MESH,
        )

    half_rows = pl.ds(
        pl.multiple_of(column * (slots * HALF), HALF), slots * HALF
    )

    def ints_piece(i):
        b = jnp.where(end == 0, n - 1 - i, i)
        return pltpu.make_async_remote_copy(
            src_ref=ints_hbm.at[
                1, half_rows, pl.ds(pl.multiple_of(b * chunk, chunk), chunk)
            ],
            dst_ref=end_ints.at[i, half_rows],
            send_sem=i_send.at[i],
            recv_sem=i_recv.at[i],
            device_id={"pair": helper},
            device_id_type=MESH,
        )

    def ints_across(i):
        return pltpu.make_async_remote_copy(
            src_ref=end_ints.at[i, half_rows],
            dst_ref=end_ints.at[i, half_rows],
            send_sem=x_send.at[i],
            recv_sem=x_recv.at[i],
            device_id={"amp": 1 - column},
            device_id_type=MESH,
        )

    pack(0)
    pl.semaphore_wait(barrier, n + 1 if proxy else n)
    for g in range(2):
        if g == 1:
            pack(1)

        @pl.loop(1, n)
        def _(off):
            if g == 0 or not proxy:
                exchange(g, off)[0].start()
            else:
                d = lax.rem(me + off, n)
                to_end_run = (d == 0) | (d == n - 1)

                @pl.when(jnp.logical_not(to_end_run))
                def _():
                    exchange(1, off)[0].start()

                @pl.when(to_end_run & (jnp.clip(d, 1, n - 2) != me))
                def _():
                    to_helper(off, d).start()

    if proxy:

        @pl.when(at_end)
        def _():
            to_helper(0, me).start()
            ints_piece(0).start()

        @pl.when(is_helper)
        def _():
            for j in range(most):
                for h in range(2):
                    pool_end[h, me * most + j] = amps[1, send_tab[1, end * (most + 1) + j], h]

    for g in range(2):
        for j in range(most):
            for h in range(2):
                pools[g][h, me * most + j] = amps[g, send_tab[g, me * (most + 1) + j], h]

    for g in range(2):
        loads[g].wait()

        @pl.loop(0, BLOCKS)
        def _(b):
            columns = pl.ds(pl.multiple_of(b * block, block), block)
            high, low = split(ints[g, :, columns].T)
            ints_hi[g, columns, :] = high
            ints_lo[g, columns, :] = low

    def send_right(g, t, src):
        return pltpu.make_async_remote_copy(
            src_ref=src,
            dst_ref=from_left.at[g, t],
            send_sem=r_send.at[g, t],
            recv_sem=r_recv.at[g, t],
            device_id={"pair": lax.rem(me + 1, n)},
            device_id_type=MESH,
        )

    def send_left(g, t, src):
        return pltpu.make_async_remote_copy(
            src_ref=src,
            dst_ref=from_right.at[g, t],
            send_sem=l_send.at[g, t],
            recv_sem=l_recv.at[g, t],
            device_id={"pair": lax.rem(me - 1 + n, n)},
            device_id_type=MESH,
        )

    def own(t):
        return pl.ds(pl.multiple_of(t * chunk, chunk), chunk)

    def gather_direct(g):
        @pl.loop(1, n)
        def _(off):
            arrive, pass_on = exchange(g, off)
            arrive.wait_recv()
            pass_on.start()

        @pl.loop(1, n)
        def _(off):
            exchange(g, off)[1].wait_recv()

    def pick_rows(row, pool, hi_ref, lo_ref):
        @pl.loop(0, slots)
        def _(k):
            where = pick_tab[row, k]
            tile = jnp.concatenate([pool[0, where], pool[1, where]], axis=0)
            high, low = split(tile)
            at = pl.ds(pl.multiple_of(k * TILE, TILE), TILE)
            hi_ref[at, :] = high
            lo_ref[at, :] = low

    def product(hi_ref, lo_ref, a_hi, a_lo, at):
        dot = functools.partial(jnp.dot, preferred_element_type=jnp.float32)
        return (
            dot(hi_ref[at, :], a_lo[...])
            + dot(lo_ref[at, :], a_hi[...])
            + dot(hi_ref[at, :], a_hi[...])
        )

    for g in range(2):
        if g == 0 or not proxy:
            gather_direct(g)
        else:

            @pl.when(is_helper)
            def _():
                @pl.loop(0, n)
                def _(home):
                    @pl.when(home != me)
                    def _():
                        to_helper_in = pltpu.make_async_remote_copy(
                            src_ref=packed.at[1, 0],
                            dst_ref=pool_end.at[core, pl.ds(home * most, most)],
                            send_sem=p_send.at[home],
                            recv_sem=p_recv.at[home],
                            device_id={"pair": end},
                            device_id_type=MESH,
                        )
                        to_helper_in.wait_recv()
                        end_pass(home).start()

                to_end().start()

            @pl.when(at_end)
            def _():
                to_end().wait_recv()
                end_share().start()
                end_share().wait_recv()

            @pl.when(jnp.logical_not(at_end))
            def _():
                gather_direct(1)

            @pl.when(is_helper)
            def _():
                @pl.loop(0, n)
                def _(home):
                    @pl.when(home != me)
                    def _():
                        end_pass(home).wait_recv()

                @pl.loop(0, n - 1)
                def _(i):
                    ints_piece(i).wait_recv()
                    ints_across(i).start()

                pick_rows(2, pool_end, end_amp_hi, end_amp_lo)

        pick_rows(g, pools[g], amp_hi.at[g], amp_lo.at[g])
        if g == 0 and proxy:

            @pl.when(at_end)
            def _():
                @pl.loop(1, n - 1)
                def _(i):
                    ints_piece(i).start()

        @pl.loop(0, BLOCKS)
        def _(i):
            b = jnp.where(me < n // 2, BLOCKS - 1 - i, i)
            at = pl.ds(pl.multiple_of(b * block, block), block)
            part[g, at, :] = product(
                ints_hi.at[g], ints_lo.at[g], amp_hi.at[g], amp_lo.at[g], at
            )
            if g == 1 and proxy:

                @pl.when(is_helper & (i < n - 1))
                def _():
                    ints_across(i).wait_recv()
                    high, low = split(end_ints[i].T)
                    end_hi[...] = high
                    end_lo[...] = low
                    part[g, at, :] = part[g, at, :] + product(
                        end_hi, end_lo, end_amp_hi, end_amp_lo, pl.ds(0, chunk)
                    )

            @pl.loop(0, per_block)
            def _(j):
                t = b * per_block + jnp.where(me < n // 2, per_block - 1 - j, j)

                @pl.when((me == first_right[g]) & (t > me))
                def _():
                    send_right(g, t, part.at[g, own(t)]).start()

                @pl.when((me == first_left[g]) & (t < me))
                def _():
                    send_left(g, t, part.at[g, own(t)]).start()

    def forward_right(g, t):
        @pl.when((t > me) & (me > first_right[g]))
        def _():
            copy = send_right(g, t, from_left.at[g, t])
            copy.wait_recv()
            from_left[g, t] = from_left[g, t] + part[g, own(t), :]
            copy.start()

    def forward_left(g, t):
        @pl.when((t < me) & (me < first_left[g]))
        def _():
            copy = send_left(g, t, from_right.at[g, t])
            copy.wait_recv()
            from_right[g, t] = from_right[g, t] + part[g, own(t), :]
            copy.start()

    for g in range(2):

        @pl.loop(0, n)
        def _(i):
            @pl.when(me < n // 2)
            def _():
                forward_right(g, n - 1 - i)
                forward_left(g, i)

            @pl.when(me >= n // 2)
            def _():
                forward_left(g, i)
                forward_right(g, n - 1 - i)

    for g in range(2):
        @pl.when(me > first_right[g])
        def _():
            send_right(g, me, from_left.at[g, me]).wait_recv()
            part[g, own(me), :] = part[g, own(me), :] + from_left[g, me]

        @pl.when(me < first_left[g])
        def _():
            send_left(g, me, from_right.at[g, me]).wait_recv()
            part[g, own(me), :] = part[g, own(me), :] + from_right[g, me]

        out[:, g, :] = part[g, own(me), :]

    for g in range(2):

        @pl.loop(1, n)
        def _(off):
            if g == 0 or not proxy:
                exchange(g, off)[0].wait_send()
                exchange(g, off)[1].wait_send()
            else:
                d = lax.rem(me + off, n)

                @pl.when(((d != 0) & (d != n - 1)) | (jnp.clip(d, 1, n - 2) != me))
                def _():
                    exchange(1, off)[0].wait_send()

                @pl.when(jnp.logical_not(at_end))
                def _():
                    exchange(1, off)[1].wait_send()

        @pl.loop(0, n)
        def _(t):
            @pl.when((t > me) & (me >= first_right[g]))
            def _():
                send_right(g, t, from_left.at[g, t]).wait_send()

            @pl.when((t < me) & (me <= first_left[g]))
            def _():
                send_left(g, t, from_right.at[g, t]).wait_send()

    if proxy:

        @pl.when(at_end)
        def _():
            to_helper(0, me).wait_send()
            end_share().wait_send()

            @pl.loop(0, n - 1)
            def _(i):
                ints_piece(i).wait_send()

        @pl.when(is_helper)
        def _():
            to_end().wait_send()

            @pl.loop(0, n)
            def _(home):
                @pl.when(home != me)
                def _():
                    end_pass(home).wait_send()

            @pl.loop(0, n - 1)
            def _(i):
                ints_across(i).wait_send()


def local(n, columns, amplitudes, integrals, tile_map, residual):
    depth, occ = amplitudes.shape[1:]
    rows = integrals.shape[2]
    slots = depth // TILE
    most = (slots + n - 1) // n
    chunk = rows // n
    proxy = n == BLOCKS and columns == 2 and chunk % 128 == 0
    smem = pl.BlockSpec(memory_space=pltpu.SMEM)
    vmem = pl.BlockSpec(memory_space=pltpu.VMEM)
    send_tab, pick_tab = pl.pallas_call(
        functools.partial(table_kernel, n, most),
        out_shape=(
            jax.ShapeDtypeStruct((2, n * (most + 1)), jnp.int32),
            jax.ShapeDtypeStruct((3, slots), jnp.int32),
        ),
        in_specs=[smem],
        out_specs=(smem, smem),
        scratch_shapes=[pltpu.SMEM((n,), jnp.int32)],
    )(tile_map)
    f32, bf16 = jnp.float32, jnp.bfloat16
    dma = pltpu.SemaphoreType.DMA
    flops = 2 * 3 * 2 * depth * rows * occ
    summed = pl.pallas_call(
        functools.partial(ladder_kernel, n, most, proxy),
        out_shape=jax.ShapeDtypeStruct((chunk, 2, occ), f32),
        in_specs=[smem, smem, vmem, pl.BlockSpec(memory_space=pl.ANY)],
        out_specs=vmem,
        scratch_shapes=[
            pltpu.VMEM((2, depth, rows), f32),
            pltpu.VMEM((2, n, most, HALF, occ), f32),
            pltpu.VMEM((2, n * most, HALF, occ), f32),
            pltpu.VMEM((2, n * most, HALF, occ), f32),
            pltpu.VMEM((2, rows, depth), bf16),
            pltpu.VMEM((2, rows, depth), bf16),
            pltpu.VMEM((2, depth, occ), bf16),
            pltpu.VMEM((2, depth, occ), bf16),
            pltpu.VMEM((2, rows, occ), f32),
            pltpu.VMEM((2, n, chunk, occ), f32),
            pltpu.VMEM((2, n, chunk, occ), f32),
            pltpu.VMEM((2, n * most, HALF, occ), f32),
            pltpu.VMEM((n - 1, depth, chunk) if proxy else (1, 8, 128), f32),
            pltpu.VMEM((chunk, depth) if proxy else (16, 128), bf16),
            pltpu.VMEM((chunk, depth) if proxy else (16, 128), bf16),
            pltpu.VMEM((depth, occ), bf16),
            pltpu.VMEM((depth, occ), bf16),
            dma((2,)),
        ]
        + [dma((2, n))] * 8
        + [dma((n,))] * 8
        + [dma((4,))],
        compiler_params=pltpu.CompilerParams(
            collective_id=0, has_side_effects=True, vmem_limit_bytes=56 * 1024 * 1024
        ),
        cost_estimate=pl.CostEstimate(
            flops=flops, bytes_accessed=4 * (integrals.size + amplitudes.size), transcendentals=0
        ),
    )(
        send_tab,
        pick_tab,
        amplitudes.reshape(2, slots, 2, HALF, occ),
        integrals,
    )
    return residual + 0.5 * summed[None]


def solution(mesh):
    placed = (
        P("groups", "pair", "amp"),
        P("groups", "pair", "rep"),
        P("groups", None),
        P("rep", "pair", "groups", "amp"),
    )
    return jax.shard_map(
        functools.partial(local, mesh.shape["pair"], mesh.shape["amp"]),
        mesh=mesh,
        in_specs=placed,
        out_specs=P("rep", "pair", "groups", "amp"),
        check_vma=False,
    )
```

```python
import functools

import jax
import jax.numpy as jnp
from jax import lax
from jax.experimental import pallas as pl
from jax.experimental.pallas import tpu as pltpu
from jax.sharding import PartitionSpec as P

TILE = 16
HALF = TILE // 2
BLOCKS = 4
MESH = pl.DeviceIdType.MESH


def table_kernel(n, most, map_ref, send_ref, pick_ref, count_ref):
    me = lax.axis_index("pair")
    slots = map_ref.shape[1] // n
    scale = ((1 << 20) + slots - 1) // slots
    low = me * slots

    for g in range(2):

        @pl.loop(0, n)
        def _(d):
            for j in range(most + 1):
                send_ref[g, d * (most + 1) + j] = 0
            found = jnp.int32(0)
            for k in range(slots):
                tile = map_ref[g, d * slots + k]
                mine = (tile >= low) & (tile < low + slots)
                send_ref[g, d * (most + 1) + found] = jnp.where(mine, tile - low, 0)
                found = found + mine.astype(jnp.int32)

        runs = [(g, me)] if g == 0 else [(1, me), (2, jnp.where(me < n // 2, 0, n - 1))]
        for row, run in runs:

            @pl.loop(0, n)
            def _(d):
                count_ref[d] = 0

            for k in range(slots):
                tile = map_ref[g, run * slots + k]
                home = lax.shift_right_logical(tile * scale, 20)
                rank = count_ref[home]
                pick_ref[row, k] = home * most + rank
                count_ref[home] = rank + 1


def split(x):
    high = x.astype(jnp.bfloat16)
    return high, (x - high.astype(jnp.float32)).astype(jnp.bfloat16)


def ladder_kernel(
    n,
    most,
    proxy,
    send_tab,
    pick_tab,
    amps,
    ints_hbm,
    out,
    ints,
    packed,
    pool0,
    pool1,
    ints_hi,
    ints_lo,
    amp_hi,
    amp_lo,
    part,
    from_left,
    from_right,
    pool_end,
    end_ints,
    end_hi,
    end_lo,
    end_amp_hi,
    end_amp_lo,
    load_sem,
    a_send,
    a_recv,
    s_send,
    s_recv,
    r_send,
    r_recv,
    l_send,
    l_recv,
    p_send,
    p_recv,
    q_send,
    q_recv,
    i_send,
    i_recv,
    x_send,
    x_recv,
    f_sem,
):
    me = lax.axis_index("pair")
    core = lax.axis_index("rep")
    column = lax.axis_index("amp")
    end = jnp.where(me < n // 2, 0, n - 1)
    at_end = me == end
    helper = jnp.clip(end, 1, n - 2)
    is_helper = me == helper
    first_right = (0, 1 if proxy else 0)
    first_left = (n - 1, n - 2 if proxy else n - 1)
    slots = amps.shape[1]
    rows = part.shape[1]
    block = rows // BLOCKS
    chunk = rows // n
    per_block = n // BLOCKS
    pools = (pool0, pool1)

    loads = [pltpu.make_async_copy(ints_hbm.at[g], ints.at[g], load_sem.at[g]) for g in range(2)]
    for load in loads:
        load.start()

    barrier = pltpu.get_barrier_semaphore()

    @pl.loop(1, n)
    def _(off):
        pl.semaphore_signal(
            barrier, inc=1, device_id={"pair": lax.rem(me + off, n)}, device_id_type=MESH
        )

    pl.semaphore_signal(barrier, inc=1, device_id={"rep": 1 - core}, device_id_type=MESH)
    if proxy:
        pl.semaphore_signal(barrier, inc=1, device_id={"amp": 1 - column}, device_id_type=MESH)

    def pack(g):
        @pl.loop(0 if proxy and g == 1 else 1, n)
        def _(off):
            d = lax.rem(me + off, n)
            for j in range(most):
                packed[g, off, j] = amps[g, send_tab[g, d * (most + 1) + j], core]

    def exchange(g, off):
        source = lax.rem(me - off + n, n)
        target = lax.rem(me + off, n)
        return (
            pltpu.make_async_remote_copy(
                src_ref=packed.at[g, off],
                dst_ref=pools[g].at[core, pl.ds(me * most, most)],
                send_sem=a_send.at[g, off],
                recv_sem=a_recv.at[g, off],
                device_id={"pair": target},
                device_id_type=MESH,
            ),
            pltpu.make_async_remote_copy(
                src_ref=pools[g].at[core, pl.ds(source * most, most)],
                dst_ref=pools[g].at[core, pl.ds(source * most, most)],
                send_sem=s_send.at[g, off],
                recv_sem=s_recv.at[g, off],
                device_id={"rep": 1 - core},
                device_id_type=MESH,
            ),
        )

    def to_helper(off, d):
        return pltpu.make_async_remote_copy(
            src_ref=packed.at[1, off],
            dst_ref=pool_end.at[core, pl.ds(me * most, most)],
            send_sem=a_send.at[1, off],
            recv_sem=p_recv.at[me],
            device_id={"pair": jnp.clip(d, 1, n - 2)},
            device_id_type=MESH,
        )

    def end_pass(home):
        rows_at = (core, pl.ds(home * most, most))
        return pltpu.make_async_remote_copy(
            src_ref=pool_end.at[rows_at],
            dst_ref=pool_end.at[rows_at],
            send_sem=q_send.at[home],
            recv_sem=q_recv.at[home],
            device_id={"rep": 1 - core},
            device_id_type=MESH,
        )

    others = (core, pl.ds(jnp.where(end == 0, most, 0), (n - 1) * most))

    def to_end():
        return pltpu.make_async_remote_copy(
            src_ref=pool_end.at[others],
            dst_ref=pool1.at[others],
            send_sem=f_sem.at[0],
            recv_sem=f_sem.at[1],
            device_id={"pair": end},
            device_id_type=MESH,
        )

    def end_share():
        return pltpu.make_async_remote_copy(
            src_ref=pool1.at[others],
            dst_ref=pool1.at[others],
            send_sem=f_sem.at[2],
            recv_sem=f_sem.at[3],
            device_id={"rep": 1 - core},
            device_id_type=MESH,
        )

    half_rows = pl.ds(
        pl.multiple_of(column * (slots * HALF), HALF), slots * HALF
    )

    def ints_piece(i):
        b = jnp.where(end == 0, n - 1 - i, i)
        return pltpu.make_async_remote_copy(
            src_ref=ints_hbm.at[
                1, half_rows, pl.ds(pl.multiple_of(b * chunk, chunk), chunk)
            ],
            dst_ref=end_ints.at[i, half_rows],
            send_sem=i_send.at[i],
            recv_sem=i_recv.at[i],
            device_id={"pair": helper},
            device_id_type=MESH,
        )

    def ints_across(i):
        return pltpu.make_async_remote_copy(
            src_ref=end_ints.at[i, half_rows],
            dst_ref=end_ints.at[i, half_rows],
            send_sem=x_send.at[i],
            recv_sem=x_recv.at[i],
            device_id={"amp": 1 - column},
            device_id_type=MESH,
        )

    order = (1, 0) if proxy else (0, 1)
    pack(order[0])
    pl.semaphore_wait(barrier, n + 1 if proxy else n)
    for step, g in enumerate(order):
        if step == 1:
            pack(g)

        @pl.loop(1, n)
        def _(off):
            if g == 0 or not proxy:
                exchange(g, off)[0].start()
            else:
                d = lax.rem(me + off, n)
                to_end_run = (d == 0) | (d == n - 1)

                @pl.when(jnp.logical_not(to_end_run))
                def _():
                    exchange(1, off)[0].start()

                @pl.when(to_end_run & (jnp.clip(d, 1, n - 2) != me))
                def _():
                    to_helper(off, d).start()

        if proxy:

            @pl.when(at_end)
            def _():
                if g == 1:
                    to_helper(0, me).start()
                ints_piece(step).start()

    if proxy:

        @pl.when(is_helper)
        def _():
            for j in range(most):
                for h in range(2):
                    pool_end[h, me * most + j] = amps[1, send_tab[1, end * (most + 1) + j], h]

    for g in range(2):
        for j in range(most):
            for h in range(2):
                pools[g][h, me * most + j] = amps[g, send_tab[g, me * (most + 1) + j], h]

    for g in range(2):
        loads[g].wait()

        @pl.loop(0, BLOCKS)
        def _(b):
            columns = pl.ds(pl.multiple_of(b * block, block), block)
            high, low = split(ints[g, :, columns].T)
            ints_hi[g, columns, :] = high
            ints_lo[g, columns, :] = low

    def send_right(g, t, src):
        return pltpu.make_async_remote_copy(
            src_ref=src,
            dst_ref=from_left.at[g, t],
            send_sem=r_send.at[g, t],
            recv_sem=r_recv.at[g, t],
            device_id={"pair": lax.rem(me + 1, n)},
            device_id_type=MESH,
        )

    def send_left(g, t, src):
        return pltpu.make_async_remote_copy(
            src_ref=src,
            dst_ref=from_right.at[g, t],
            send_sem=l_send.at[g, t],
            recv_sem=l_recv.at[g, t],
            device_id={"pair": lax.rem(me - 1 + n, n)},
            device_id_type=MESH,
        )

    def own(t):
        return pl.ds(pl.multiple_of(t * chunk, chunk), chunk)

    def gather_direct(g):
        @pl.loop(1, n)
        def _(off):
            arrive, pass_on = exchange(g, off)
            arrive.wait_recv()
            pass_on.start()

        @pl.loop(1, n)
        def _(off):
            exchange(g, off)[1].wait_recv()

    def pick_rows(row, pool, hi_ref, lo_ref):
        @pl.loop(0, slots)
        def _(k):
            where = pick_tab[row, k]
            tile = jnp.concatenate([pool[0, where], pool[1, where]], axis=0)
            high, low = split(tile)
            at = pl.ds(pl.multiple_of(k * TILE, TILE), TILE)
            hi_ref[at, :] = high
            lo_ref[at, :] = low

    def product(hi_ref, lo_ref, a_hi, a_lo, at):
        dot = functools.partial(jnp.dot, preferred_element_type=jnp.float32)
        return (
            dot(hi_ref[at, :], a_lo[...])
            + dot(lo_ref[at, :], a_hi[...])
            + dot(hi_ref[at, :], a_hi[...])
        )

    def near_first(i):
        return jnp.where(me < n // 2, BLOCKS - 1 - i, i)

    def send_first(g, i):
        @pl.loop(0, per_block)
        def _(j):
            t = near_first(i) * per_block + jnp.where(me < n // 2, per_block - 1 - j, j)

            @pl.when((me == first_right[g]) & (t > me))
            def _():
                send_right(g, t, part.at[g, own(t)]).start()

            @pl.when((me == first_left[g]) & (t < me))
            def _():
                send_left(g, t, part.at[g, own(t)]).start()

    def multiply(g, b):
        at = pl.ds(pl.multiple_of(b * block, block), block)
        part[g, at, :] = product(ints_hi.at[g], ints_lo.at[g], amp_hi.at[g], amp_lo.at[g], at)

    def choose(g):
        pick_rows(g, pools[g], amp_hi.at[g], amp_lo.at[g])

    def multiply_end(i):
        ints_across(i).wait_recv()
        at = own(near_first(i))
        high, low = split(end_ints[i].T)
        end_hi[...] = high
        end_lo[...] = low
        part[1, at, :] = part[1, at, :] + product(
            end_hi, end_lo, end_amp_hi, end_amp_lo, pl.ds(0, chunk)
        )

    def take_piece(i):
        ints_piece(i).wait_recv()
        ints_across(i).start()

    if proxy:

        @pl.when(at_end)
        def _():
            gather_direct(0)
            choose(0)

            @pl.loop(0, n)
            def _(i):
                @pl.when(i == n - 2)
                def _():
                    @pl.loop(2, n - 1)
                    def _(piece):
                        ints_piece(piece).start()

                multiply(0, near_first(i))
                send_first(0, i)

            to_end().wait_recv()
            end_share().start()
            end_share().wait_recv()
            choose(1)
            multiply(1, me)

        @pl.when(is_helper)
        def _():
            @pl.loop(0, n)
            def _(home):
                @pl.when(home != me)
                def _():
                    to_helper_in = pltpu.make_async_remote_copy(
                        src_ref=packed.at[1, 0],
                        dst_ref=pool_end.at[core, pl.ds(home * most, most)],
                        send_sem=p_send.at[home],
                        recv_sem=p_recv.at[home],
                        device_id={"pair": end},
                        device_id_type=MESH,
                    )
                    to_helper_in.wait_recv()
                    end_pass(home).start()

            gather_direct(1)

            @pl.loop(0, n)
            def _(home):
                @pl.when(home != me)
                def _():
                    end_pass(home).wait_recv()

            choose(1)
            pick_rows(2, pool_end, end_amp_hi, end_amp_lo)
            take_piece(0)

            @pl.loop(0, n)
            def _(i):
                multiply(1, near_first(i))

            gather_direct(0)
            to_end().start()
            choose(0)

            @pl.loop(0, n)
            def _(i):
                multiply(0, near_first(i))

            @pl.loop(0, n - 2)
            def _(i):
                @pl.when(i > 0)
                def _():
                    take_piece(i)

                multiply_end(i)
                send_first(1, i)
    else:
        for g in range(2):
            gather_direct(g)
            choose(g)

            @pl.loop(0, BLOCKS)
            def _(i):
                multiply(g, near_first(i))
                send_first(g, i)

    def forward_right(g, t):
        @pl.when((t > me) & (me > first_right[g]))
        def _():
            copy = send_right(g, t, from_left.at[g, t])
            copy.wait_recv()
            from_left[g, t] = from_left[g, t] + part[g, own(t), :]
            copy.start()

    def forward_left(g, t):
        @pl.when((t < me) & (me < first_left[g]))
        def _():
            copy = send_left(g, t, from_right.at[g, t])
            copy.wait_recv()
            from_right[g, t] = from_right[g, t] + part[g, own(t), :]
            copy.start()

    for g in range(2):

        @pl.loop(0, n)
        def _(i):
            @pl.when(me < n // 2)
            def _():
                forward_right(g, n - 1 - i)
                forward_left(g, i)

            @pl.when(me >= n // 2)
            def _():
                forward_left(g, i)
                forward_right(g, n - 1 - i)

    if proxy:

        @pl.when(is_helper)
        def _():
            take_piece(n - 2)
            multiply_end(n - 2)

    for g in range(2):

        @pl.when(me > first_right[g])
        def _():
            send_right(g, me, from_left.at[g, me]).wait_recv()
            part[g, own(me), :] = part[g, own(me), :] + from_left[g, me]

        @pl.when(me < first_left[g])
        def _():
            send_left(g, me, from_right.at[g, me]).wait_recv()
            part[g, own(me), :] = part[g, own(me), :] + from_right[g, me]

        out[:, g, :] = part[g, own(me), :]

    for g in range(2):

        @pl.loop(1, n)
        def _(off):
            if g == 0 or not proxy:
                exchange(g, off)[0].wait_send()
                exchange(g, off)[1].wait_send()
            else:
                d = lax.rem(me + off, n)

                @pl.when(((d != 0) & (d != n - 1)) | (jnp.clip(d, 1, n - 2) != me))
                def _():
                    exchange(1, off)[0].wait_send()

                @pl.when(jnp.logical_not(at_end))
                def _():
                    exchange(1, off)[1].wait_send()

        @pl.loop(0, n)
        def _(t):
            @pl.when((t > me) & (me >= first_right[g]))
            def _():
                send_right(g, t, from_left.at[g, t]).wait_send()

            @pl.when((t < me) & (me <= first_left[g]))
            def _():
                send_left(g, t, from_right.at[g, t]).wait_send()

    if proxy:

        @pl.when(at_end)
        def _():
            to_helper(0, me).wait_send()
            end_share().wait_send()

            @pl.loop(0, n - 1)
            def _(i):
                ints_piece(i).wait_send()

        @pl.when(is_helper)
        def _():
            to_end().wait_send()

            @pl.loop(0, n)
            def _(home):
                @pl.when(home != me)
                def _():
                    end_pass(home).wait_send()

            @pl.loop(0, n - 1)
            def _(i):
                ints_across(i).wait_send()


def local(n, columns, amplitudes, integrals, tile_map, residual):
    depth, occ = amplitudes.shape[1:]
    rows = integrals.shape[2]
    slots = depth // TILE
    most = (slots + n - 1) // n
    chunk = rows // n
    proxy = n == BLOCKS and columns == 2 and chunk % 128 == 0
    smem = pl.BlockSpec(memory_space=pltpu.SMEM)
    vmem = pl.BlockSpec(memory_space=pltpu.VMEM)
    send_tab, pick_tab = pl.pallas_call(
        functools.partial(table_kernel, n, most),
        out_shape=(
            jax.ShapeDtypeStruct((2, n * (most + 1)), jnp.int32),
            jax.ShapeDtypeStruct((3, slots), jnp.int32),
        ),
        in_specs=[smem],
        out_specs=(smem, smem),
        scratch_shapes=[pltpu.SMEM((n,), jnp.int32)],
    )(tile_map)
    f32, bf16 = jnp.float32, jnp.bfloat16
    dma = pltpu.SemaphoreType.DMA
    flops = 2 * 3 * 2 * depth * rows * occ
    summed = pl.pallas_call(
        functools.partial(ladder_kernel, n, most, proxy),
        out_shape=jax.ShapeDtypeStruct((chunk, 2, occ), f32),
        in_specs=[smem, smem, vmem, pl.BlockSpec(memory_space=pl.ANY)],
        out_specs=vmem,
        scratch_shapes=[
            pltpu.VMEM((2, depth, rows), f32),
            pltpu.VMEM((2, n, most, HALF, occ), f32),
            pltpu.VMEM((2, n * most, HALF, occ), f32),
            pltpu.VMEM((2, n * most, HALF, occ), f32),
            pltpu.VMEM((2, rows, depth), bf16),
            pltpu.VMEM((2, rows, depth), bf16),
            pltpu.VMEM((2, depth, occ), bf16),
            pltpu.VMEM((2, depth, occ), bf16),
            pltpu.VMEM((2, rows, occ), f32),
            pltpu.VMEM((2, n, chunk, occ), f32),
            pltpu.VMEM((2, n, chunk, occ), f32),
            pltpu.VMEM((2, n * most, HALF, occ), f32),
            pltpu.VMEM((n - 1, depth, chunk) if proxy else (1, 8, 128), f32),
            pltpu.VMEM((chunk, depth) if proxy else (16, 128), bf16),
            pltpu.VMEM((chunk, depth) if proxy else (16, 128), bf16),
            pltpu.VMEM((depth, occ), bf16),
            pltpu.VMEM((depth, occ), bf16),
            dma((2,)),
        ]
        + [dma((2, n))] * 8
        + [dma((n,))] * 8
        + [dma((4,))],
        compiler_params=pltpu.CompilerParams(
            collective_id=0, has_side_effects=True, vmem_limit_bytes=56 * 1024 * 1024
        ),
        cost_estimate=pl.CostEstimate(
            flops=flops, bytes_accessed=4 * (integrals.size + amplitudes.size), transcendentals=0
        ),
    )(
        send_tab,
        pick_tab,
        amplitudes.reshape(2, slots, 2, HALF, occ),
        integrals,
    )
    return residual + 0.5 * summed[None]


def solution(mesh):
    placed = (
        P("groups", "pair", "amp"),
        P("groups", "pair", "rep"),
        P("groups", None),
        P("rep", "pair", "groups", "amp"),
    )
    return jax.shard_map(
        functools.partial(local, mesh.shape["pair"], mesh.shape["amp"]),
        mesh=mesh,
        in_specs=placed,
        out_specs=P("rep", "pair", "groups", "amp"),
        check_vma=False,
    )
```

```python
import functools

import jax
import jax.numpy as jnp
from jax import lax
from jax.experimental import pallas as pl
from jax.experimental.pallas import tpu as pltpu
from jax.sharding import PartitionSpec as P

TILE = 16
HALF = TILE // 2
BLOCKS = 4
MESH = pl.DeviceIdType.MESH


def table_kernel(n, most, map_ref, send_ref, pick_ref, count_ref):
    me = lax.axis_index("pair")
    slots = map_ref.shape[1] // n
    scale = ((1 << 20) + slots - 1) // slots
    low = me * slots

    for g in range(2):

        @pl.loop(0, n)
        def _(d):
            for j in range(most + 1):
                send_ref[g, d * (most + 1) + j] = 0
            found = jnp.int32(0)
            for k in range(slots):
                tile = map_ref[g, d * slots + k]
                mine = (tile >= low) & (tile < low + slots)
                send_ref[g, d * (most + 1) + found] = jnp.where(mine, tile - low, 0)
                found = found + mine.astype(jnp.int32)

        runs = [(g, me)] if g == 0 else [(1, me), (2, jnp.where(me < n // 2, 0, n - 1))]
        for row, run in runs:

            @pl.loop(0, n)
            def _(d):
                count_ref[d] = 0

            for k in range(slots):
                tile = map_ref[g, run * slots + k]
                home = lax.shift_right_logical(tile * scale, 20)
                rank = count_ref[home]
                pick_ref[row, k] = home * most + rank
                count_ref[home] = rank + 1


def split(x):
    high = x.astype(jnp.bfloat16)
    return high, (x - high.astype(jnp.float32)).astype(jnp.bfloat16)


def ladder_kernel(
    n,
    most,
    proxy,
    send_tab,
    pick_tab,
    amps,
    ints_hbm,
    residual,
    out,
    ints,
    packed,
    pool0,
    pool1,
    ints_hi,
    ints_lo,
    amp_hi,
    amp_lo,
    part,
    from_left,
    from_right,
    pool_end,
    end_ints,
    end_hi,
    end_lo,
    end_amp_hi,
    end_amp_lo,
    load_sem,
    a_send,
    a_recv,
    s_send,
    s_recv,
    r_send,
    r_recv,
    l_send,
    l_recv,
    p_send,
    p_recv,
    q_send,
    q_recv,
    i_send,
    i_recv,
    x_send,
    x_recv,
    f_sem,
):
    me = lax.axis_index("pair")
    core = lax.axis_index("rep")
    column = lax.axis_index("amp")
    end = jnp.where(me < n // 2, 0, n - 1)
    at_end = me == end
    helper = jnp.clip(end, 1, n - 2)
    is_helper = me == helper
    first_right = (0, 1 if proxy else 0)
    first_left = (n - 1, n - 2 if proxy else n - 1)
    slots = amps.shape[1]
    rows = part.shape[1]
    block = rows // BLOCKS
    chunk = rows // n
    per_block = n // BLOCKS
    pools = (pool0, pool1)

    loads = [pltpu.make_async_copy(ints_hbm.at[g], ints.at[g], load_sem.at[g]) for g in range(2)]
    for load in loads:
        load.start()

    barrier = pltpu.get_barrier_semaphore()

    @pl.loop(1, n)
    def _(off):
        pl.semaphore_signal(
            barrier, inc=1, device_id={"pair": lax.rem(me + off, n)}, device_id_type=MESH
        )

    pl.semaphore_signal(barrier, inc=1, device_id={"rep": 1 - core}, device_id_type=MESH)
    if proxy:
        pl.semaphore_signal(barrier, inc=1, device_id={"amp": 1 - column}, device_id_type=MESH)

    def pack(g):
        @pl.loop(0 if proxy and g == 1 else 1, n)
        def _(off):
            d = lax.rem(me + off, n)
            for j in range(most):
                packed[g, off, j] = amps[g, send_tab[g, d * (most + 1) + j], core]

    def exchange(g, off):
        source = lax.rem(me - off + n, n)
        target = lax.rem(me + off, n)
        return (
            pltpu.make_async_remote_copy(
                src_ref=packed.at[g, off],
                dst_ref=pools[g].at[core, pl.ds(me * most, most)],
                send_sem=a_send.at[g, off],
                recv_sem=a_recv.at[g, off],
                device_id={"pair": target},
                device_id_type=MESH,
            ),
            pltpu.make_async_remote_copy(
                src_ref=pools[g].at[core, pl.ds(source * most, most)],
                dst_ref=pools[g].at[core, pl.ds(source * most, most)],
                send_sem=s_send.at[g, off],
                recv_sem=s_recv.at[g, off],
                device_id={"rep": 1 - core},
                device_id_type=MESH,
            ),
        )

    def to_helper(off, d):
        return pltpu.make_async_remote_copy(
            src_ref=packed.at[1, off],
            dst_ref=pool_end.at[core, pl.ds(me * most, most)],
            send_sem=a_send.at[1, off],
            recv_sem=p_recv.at[me],
            device_id={"pair": jnp.clip(d, 1, n - 2)},
            device_id_type=MESH,
        )

    def end_pass(home):
        rows_at = (core, pl.ds(home * most, most))
        return pltpu.make_async_remote_copy(
            src_ref=pool_end.at[rows_at],
            dst_ref=pool_end.at[rows_at],
            send_sem=q_send.at[home],
            recv_sem=q_recv.at[home],
            device_id={"rep": 1 - core},
            device_id_type=MESH,
        )

    others = (core, pl.ds(jnp.where(end == 0, most, 0), (n - 1) * most))

    def to_end():
        return pltpu.make_async_remote_copy(
            src_ref=pool_end.at[others],
            dst_ref=pool1.at[others],
            send_sem=f_sem.at[0],
            recv_sem=f_sem.at[1],
            device_id={"pair": end},
            device_id_type=MESH,
        )

    def end_share():
        return pltpu.make_async_remote_copy(
            src_ref=pool1.at[others],
            dst_ref=pool1.at[others],
            send_sem=f_sem.at[2],
            recv_sem=f_sem.at[3],
            device_id={"rep": 1 - core},
            device_id_type=MESH,
        )

    half_rows = pl.ds(
        pl.multiple_of(column * (slots * HALF), HALF), slots * HALF
    )

    def ints_piece(i):
        b = jnp.where(end == 0, n - 1 - i, i)
        return pltpu.make_async_remote_copy(
            src_ref=ints_hbm.at[
                1, half_rows, pl.ds(pl.multiple_of(b * chunk, chunk), chunk)
            ],
            dst_ref=end_ints.at[i, half_rows],
            send_sem=i_send.at[i],
            recv_sem=i_recv.at[i],
            device_id={"pair": helper},
            device_id_type=MESH,
        )

    def ints_across(i):
        return pltpu.make_async_remote_copy(
            src_ref=end_ints.at[i, half_rows],
            dst_ref=end_ints.at[i, half_rows],
            send_sem=x_send.at[i],
            recv_sem=x_recv.at[i],
            device_id={"amp": 1 - column},
            device_id_type=MESH,
        )

    order = (1, 0) if proxy else (0, 1)
    pack(order[0])
    pl.semaphore_wait(barrier, n + 1 if proxy else n)
    for step, g in enumerate(order):
        if step == 1:
            pack(g)

        @pl.loop(1, n)
        def _(off):
            if g == 0 or not proxy:
                exchange(g, off)[0].start()
            else:
                d = lax.rem(me + off, n)
                to_end_run = (d == 0) | (d == n - 1)

                @pl.when(jnp.logical_not(to_end_run))
                def _():
                    exchange(1, off)[0].start()

                @pl.when(to_end_run & (jnp.clip(d, 1, n - 2) != me))
                def _():
                    to_helper(off, d).start()

        if proxy:

            @pl.when(at_end)
            def _():
                if g == 1:
                    to_helper(0, me).start()
                for i in (range(1, n - 1) if step == 1 else range(1)):
                    ints_piece(i).start()

    if proxy:

        @pl.when(is_helper)
        def _():
            for j in range(most):
                for h in range(2):
                    pool_end[h, me * most + j] = amps[1, send_tab[1, end * (most + 1) + j], h]

    for g in range(2):
        for j in range(most):
            for h in range(2):
                pools[g][h, me * most + j] = amps[g, send_tab[g, me * (most + 1) + j], h]

    for g in range(2):
        loads[g].wait()

        @pl.loop(0, BLOCKS)
        def _(b):
            columns = pl.ds(pl.multiple_of(b * block, block), block)
            high, low = split(ints[g, :, columns].T)
            ints_hi[g, columns, :] = high
            ints_lo[g, columns, :] = low

    def send_right(g, t, src):
        return pltpu.make_async_remote_copy(
            src_ref=src,
            dst_ref=from_left.at[g, t],
            send_sem=r_send.at[g, t],
            recv_sem=r_recv.at[g, t],
            device_id={"pair": lax.rem(me + 1, n)},
            device_id_type=MESH,
        )

    def send_left(g, t, src):
        return pltpu.make_async_remote_copy(
            src_ref=src,
            dst_ref=from_right.at[g, t],
            send_sem=l_send.at[g, t],
            recv_sem=l_recv.at[g, t],
            device_id={"pair": lax.rem(me - 1 + n, n)},
            device_id_type=MESH,
        )

    def own(t):
        return pl.ds(pl.multiple_of(t * chunk, chunk), chunk)

    def gather_direct(g):
        @pl.loop(1, n)
        def _(off):
            arrive, pass_on = exchange(g, off)
            arrive.wait_recv()
            pass_on.start()

        @pl.loop(1, n)
        def _(off):
            exchange(g, off)[1].wait_recv()

    def pick_rows(row, pool, hi_ref, lo_ref):
        @pl.loop(0, slots)
        def _(k):
            where = pick_tab[row, k]
            tile = jnp.concatenate([pool[0, where], pool[1, where]], axis=0)
            high, low = split(tile)
            at = pl.ds(pl.multiple_of(k * TILE, TILE), TILE)
            hi_ref[at, :] = high
            lo_ref[at, :] = low

    def product(hi_ref, lo_ref, a_hi, a_lo, at):
        dot = functools.partial(jnp.dot, preferred_element_type=jnp.float32)
        return (
            dot(hi_ref[at, :], a_lo[...])
            + dot(lo_ref[at, :], a_hi[...])
            + dot(hi_ref[at, :], a_hi[...])
        )

    def near_first(i):
        return jnp.where(me < n // 2, BLOCKS - 1 - i, i)

    def send_first(g, i):
        @pl.loop(0, per_block)
        def _(j):
            t = near_first(i) * per_block + jnp.where(me < n // 2, per_block - 1 - j, j)

            @pl.when((me == first_right[g]) & (t > me))
            def _():
                send_right(g, t, part.at[g, own(t)]).start()

            @pl.when((me == first_left[g]) & (t < me))
            def _():
                send_left(g, t, part.at[g, own(t)]).start()

    def multiply(g, b):
        at = pl.ds(pl.multiple_of(b * block, block), block)
        part[g, at, :] = product(ints_hi.at[g], ints_lo.at[g], amp_hi.at[g], amp_lo.at[g], at)

    def choose(g):
        pick_rows(g, pools[g], amp_hi.at[g], amp_lo.at[g])

    def multiply_end(i):
        ints_across(i).wait_recv()
        at = own(near_first(i))
        high, low = split(end_ints[i].T)
        end_hi[...] = high
        end_lo[...] = low
        part[1, at, :] = part[1, at, :] + product(
            end_hi, end_lo, end_amp_hi, end_amp_lo, pl.ds(0, chunk)
        )

    def take_piece(i):
        ints_piece(i).wait_recv()
        ints_across(i).start()

    if proxy:

        @pl.when(at_end)
        def _():
            gather_direct(0)
            choose(0)

            @pl.loop(0, n)
            def _(i):
                multiply(0, near_first(i))
                send_first(0, i)

            to_end().wait_recv()
            end_share().start()
            end_share().wait_recv()
            choose(1)
            multiply(1, me)

        @pl.when(is_helper)
        def _():
            @pl.loop(0, n)
            def _(home):
                @pl.when(home != me)
                def _():
                    to_helper_in = pltpu.make_async_remote_copy(
                        src_ref=packed.at[1, 0],
                        dst_ref=pool_end.at[core, pl.ds(home * most, most)],
                        send_sem=p_send.at[home],
                        recv_sem=p_recv.at[home],
                        device_id={"pair": end},
                        device_id_type=MESH,
                    )
                    to_helper_in.wait_recv()
                    end_pass(home).start()

            gather_direct(1)

            @pl.loop(0, n)
            def _(home):
                @pl.when(home != me)
                def _():
                    end_pass(home).wait_recv()

            choose(1)
            pick_rows(2, pool_end, end_amp_hi, end_amp_lo)
            take_piece(0)

            @pl.loop(0, n)
            def _(i):
                multiply(1, near_first(i))

            multiply_end(0)
            send_first(1, 0)
            gather_direct(0)
            to_end().start()
            choose(0)

            @pl.loop(0, n)
            def _(i):
                multiply(0, near_first(i))

            @pl.loop(1, n - 2)
            def _(i):
                take_piece(i)
                multiply_end(i)
                send_first(1, i)
    else:
        for g in range(2):
            gather_direct(g)
            choose(g)

            @pl.loop(0, BLOCKS)
            def _(i):
                multiply(g, near_first(i))
                send_first(g, i)

    def forward_right(g, t):
        @pl.when((t > me) & (me > first_right[g]))
        def _():
            copy = send_right(g, t, from_left.at[g, t])
            copy.wait_recv()
            from_left[g, t] = from_left[g, t] + part[g, own(t), :]
            copy.start()

    def forward_left(g, t):
        @pl.when((t < me) & (me < first_left[g]))
        def _():
            copy = send_left(g, t, from_right.at[g, t])
            copy.wait_recv()
            from_right[g, t] = from_right[g, t] + part[g, own(t), :]
            copy.start()

    for g in range(2):

        @pl.loop(0, n)
        def _(i):
            @pl.when(me < n // 2)
            def _():
                forward_right(g, n - 1 - i)
                forward_left(g, i)

            @pl.when(me >= n // 2)
            def _():
                forward_left(g, i)
                forward_right(g, n - 1 - i)

    if proxy:

        @pl.when(is_helper)
        def _():
            take_piece(n - 2)
            multiply_end(n - 2)

    for g in range(2):

        @pl.when(me > first_right[g])
        def _():
            send_right(g, me, from_left.at[g, me]).wait_recv()
            part[g, own(me), :] = part[g, own(me), :] + from_left[g, me]

        @pl.when(me < first_left[g])
        def _():
            send_left(g, me, from_right.at[g, me]).wait_recv()
            part[g, own(me), :] = part[g, own(me), :] + from_right[g, me]

        out[:, g, :] = residual[:, g, :] + 0.5 * part[g, own(me), :]

    for g in range(2):

        @pl.loop(1, n)
        def _(off):
            if g == 0 or not proxy:
                exchange(g, off)[0].wait_send()
                exchange(g, off)[1].wait_send()
            else:
                d = lax.rem(me + off, n)

                @pl.when(((d != 0) & (d != n - 1)) | (jnp.clip(d, 1, n - 2) != me))
                def _():
                    exchange(1, off)[0].wait_send()

                @pl.when(jnp.logical_not(at_end))
                def _():
                    exchange(1, off)[1].wait_send()

        @pl.loop(0, n)
        def _(t):
            @pl.when((t > me) & (me >= first_right[g]))
            def _():
                send_right(g, t, from_left.at[g, t]).wait_send()

            @pl.when((t < me) & (me <= first_left[g]))
            def _():
                send_left(g, t, from_right.at[g, t]).wait_send()

    if proxy:

        @pl.when(at_end)
        def _():
            to_helper(0, me).wait_send()
            end_share().wait_send()

            @pl.loop(0, n - 1)
            def _(i):
                ints_piece(i).wait_send()

        @pl.when(is_helper)
        def _():
            to_end().wait_send()

            @pl.loop(0, n)
            def _(home):
                @pl.when(home != me)
                def _():
                    end_pass(home).wait_send()

            @pl.loop(0, n - 1)
            def _(i):
                ints_across(i).wait_send()


def local(n, columns, amplitudes, integrals, tile_map, residual):
    depth, occ = amplitudes.shape[1:]
    rows = integrals.shape[2]
    slots = depth // TILE
    most = (slots + n - 1) // n
    chunk = rows // n
    proxy = n == BLOCKS and columns == 2 and chunk % 128 == 0
    smem = pl.BlockSpec(memory_space=pltpu.SMEM)
    vmem = pl.BlockSpec(memory_space=pltpu.VMEM)
    send_tab, pick_tab = pl.pallas_call(
        functools.partial(table_kernel, n, most),
        out_shape=(
            jax.ShapeDtypeStruct((2, n * (most + 1)), jnp.int32),
            jax.ShapeDtypeStruct((3, slots), jnp.int32),
        ),
        in_specs=[smem],
        out_specs=(smem, smem),
        scratch_shapes=[pltpu.SMEM((n,), jnp.int32)],
    )(tile_map)
    f32, bf16 = jnp.float32, jnp.bfloat16
    dma = pltpu.SemaphoreType.DMA
    flops = 2 * 3 * 2 * depth * rows * occ
    summed = pl.pallas_call(
        functools.partial(ladder_kernel, n, most, proxy),
        out_shape=jax.ShapeDtypeStruct((chunk, 2, occ), f32),
        in_specs=[smem, smem, vmem, pl.BlockSpec(memory_space=pl.ANY), vmem],
        out_specs=vmem,
        scratch_shapes=[
            pltpu.VMEM((2, depth, rows), f32),
            pltpu.VMEM((2, n, most, HALF, occ), f32),
            pltpu.VMEM((2, n * most, HALF, occ), f32),
            pltpu.VMEM((2, n * most, HALF, occ), f32),
            pltpu.VMEM((2, rows, depth), bf16),
            pltpu.VMEM((2, rows, depth), bf16),
            pltpu.VMEM((2, depth, occ), bf16),
            pltpu.VMEM((2, depth, occ), bf16),
            pltpu.VMEM((2, rows, occ), f32),
            pltpu.VMEM((2, n, chunk, occ), f32),
            pltpu.VMEM((2, n, chunk, occ), f32),
            pltpu.VMEM((2, n * most, HALF, occ), f32),
            pltpu.VMEM((n - 1, depth, chunk) if proxy else (1, 8, 128), f32),
            pltpu.VMEM((chunk, depth) if proxy else (16, 128), bf16),
            pltpu.VMEM((chunk, depth) if proxy else (16, 128), bf16),
            pltpu.VMEM((depth, occ), bf16),
            pltpu.VMEM((depth, occ), bf16),
            dma((2,)),
        ]
        + [dma((2, n))] * 8
        + [dma((n,))] * 8
        + [dma((4,))],
        compiler_params=pltpu.CompilerParams(
            collective_id=0, has_side_effects=True, vmem_limit_bytes=56 * 1024 * 1024
        ),
        cost_estimate=pl.CostEstimate(
            flops=flops, bytes_accessed=4 * (integrals.size + amplitudes.size), transcendentals=0
        ),
    )(
        send_tab,
        pick_tab,
        amplitudes.reshape(2, slots, 2, HALF, occ),
        integrals,
        residual[0],
    )
    return summed[None]


def solution(mesh):
    placed = (
        P("groups", "pair", "amp"),
        P("groups", "pair", "rep"),
        P("groups", None),
        P("rep", "pair", "groups", "amp"),
    )
    return jax.shard_map(
        functools.partial(local, mesh.shape["pair"], mesh.shape["amp"]),
        mesh=mesh,
        in_specs=placed,
        out_specs=P("rep", "pair", "groups", "amp"),
        check_vma=False,
    )
```

```python
import functools

import jax
import jax.numpy as jnp
from jax import lax
from jax.experimental import pallas as pl
from jax.experimental.pallas import tpu as pltpu
from jax.sharding import PartitionSpec as P

TILE = 16
HALF = TILE // 2
BLOCKS = 4
MESH = pl.DeviceIdType.MESH


def table_kernel(n, most, map_ref, send_ref, pick_ref, count_ref):
    me = lax.axis_index("pair")
    slots = map_ref.shape[1] // n
    scale = ((1 << 20) + slots - 1) // slots
    low = me * slots

    for g in range(2):

        @pl.loop(0, n)
        def _(d):
            for j in range(most + 1):
                send_ref[g, d * (most + 1) + j] = 0
            found = jnp.int32(0)
            for k in range(slots):
                tile = map_ref[g, d * slots + k]
                mine = (tile >= low) & (tile < low + slots)
                send_ref[g, d * (most + 1) + found] = jnp.where(mine, tile - low, 0)
                found = found + mine.astype(jnp.int32)

        runs = [(g, me)] if g == 0 else [(1, me), (2, jnp.where(me < n // 2, 0, n - 1))]
        for row, run in runs:

            @pl.loop(0, n)
            def _(d):
                count_ref[d] = 0

            for k in range(slots):
                tile = map_ref[g, run * slots + k]
                home = lax.shift_right_logical(tile * scale, 20)
                rank = count_ref[home]
                pick_ref[row, k] = home * most + rank
                count_ref[home] = rank + 1


def split(x):
    high = x.astype(jnp.bfloat16)
    return high, (x - high.astype(jnp.float32)).astype(jnp.bfloat16)


def ladder_kernel(
    n,
    most,
    proxy,
    send_tab,
    pick_tab,
    amps,
    ints_hbm,
    residual,
    out,
    ints,
    packed,
    pool0,
    pool1,
    ints_hi,
    ints_lo,
    amp_hi,
    amp_lo,
    part,
    from_left,
    from_right,
    pool_end,
    end_ints,
    end_hi,
    end_lo,
    end_amp_hi,
    end_amp_lo,
    load_sem,
    a_send,
    a_recv,
    s_send,
    s_recv,
    r_send,
    r_recv,
    l_send,
    l_recv,
    p_send,
    p_recv,
    q_send,
    q_recv,
    i_send,
    i_recv,
    x_send,
    x_recv,
    f_sem,
):
    me = lax.axis_index("pair")
    core = lax.axis_index("rep")
    column = lax.axis_index("amp")
    end = jnp.where(me < n // 2, 0, n - 1)
    at_end = me == end
    helper = jnp.clip(end, 1, n - 2)
    is_helper = me == helper
    first_right = (0, 1 if proxy else 0)
    first_left = (n - 1, n - 2 if proxy else n - 1)
    slots = amps.shape[1]
    rows = part.shape[1]
    block = rows // BLOCKS
    chunk = rows // n
    per_block = n // BLOCKS
    pools = (pool0, pool1)

    loads = [pltpu.make_async_copy(ints_hbm.at[g], ints.at[g], load_sem.at[g]) for g in range(2)]
    for load in loads:
        load.start()

    barrier = pltpu.get_barrier_semaphore()

    @pl.loop(1, n)
    def _(off):
        pl.semaphore_signal(
            barrier, inc=1, device_id={"pair": lax.rem(me + off, n)}, device_id_type=MESH
        )

    pl.semaphore_signal(barrier, inc=1, device_id={"rep": 1 - core}, device_id_type=MESH)
    if proxy:
        pl.semaphore_signal(barrier, inc=1, device_id={"amp": 1 - column}, device_id_type=MESH)

    def pack(g):
        @pl.loop(0 if proxy and g == 1 else 1, n)
        def _(off):
            d = lax.rem(me + off, n)
            for j in range(most):
                packed[g, off, j] = amps[g, send_tab[g, d * (most + 1) + j], core]

    def exchange(g, off):
        source = lax.rem(me - off + n, n)
        target = lax.rem(me + off, n)
        return (
            pltpu.make_async_remote_copy(
                src_ref=packed.at[g, off],
                dst_ref=pools[g].at[core, pl.ds(me * most, most)],
                send_sem=a_send.at[g, off],
                recv_sem=a_recv.at[g, off],
                device_id={"pair": target},
                device_id_type=MESH,
            ),
            pltpu.make_async_remote_copy(
                src_ref=pools[g].at[core, pl.ds(source * most, most)],
                dst_ref=pools[g].at[core, pl.ds(source * most, most)],
                send_sem=s_send.at[g, off],
                recv_sem=s_recv.at[g, off],
                device_id={"rep": 1 - core},
                device_id_type=MESH,
            ),
        )

    def to_helper(off, d):
        return pltpu.make_async_remote_copy(
            src_ref=packed.at[1, off],
            dst_ref=pool_end.at[core, pl.ds(me * most, most)],
            send_sem=a_send.at[1, off],
            recv_sem=p_recv.at[me],
            device_id={"pair": jnp.clip(d, 1, n - 2)},
            device_id_type=MESH,
        )

    def end_pass(home):
        rows_at = (core, pl.ds(home * most, most))
        return pltpu.make_async_remote_copy(
            src_ref=pool_end.at[rows_at],
            dst_ref=pool_end.at[rows_at],
            send_sem=q_send.at[home],
            recv_sem=q_recv.at[home],
            device_id={"rep": 1 - core},
            device_id_type=MESH,
        )

    others = (core, pl.ds(jnp.where(end == 0, most, 0), (n - 1) * most))

    def to_end():
        return pltpu.make_async_remote_copy(
            src_ref=pool_end.at[others],
            dst_ref=pool1.at[others],
            send_sem=f_sem.at[0],
            recv_sem=f_sem.at[1],
            device_id={"pair": end},
            device_id_type=MESH,
        )

    def end_share():
        return pltpu.make_async_remote_copy(
            src_ref=pool1.at[others],
            dst_ref=pool1.at[others],
            send_sem=f_sem.at[2],
            recv_sem=f_sem.at[3],
            device_id={"rep": 1 - core},
            device_id_type=MESH,
        )

    half_rows = pl.ds(
        pl.multiple_of(column * (slots * HALF), HALF), slots * HALF
    )

    def ints_piece(i):
        b = jnp.where(end == 0, n - 1 - i, i)
        return pltpu.make_async_remote_copy(
            src_ref=ints_hbm.at[
                1, half_rows, pl.ds(pl.multiple_of(b * chunk, chunk), chunk)
            ],
            dst_ref=end_ints.at[i, half_rows],
            send_sem=i_send.at[i],
            recv_sem=i_recv.at[i],
            device_id={"pair": helper},
            device_id_type=MESH,
        )

    def ints_across(i):
        return pltpu.make_async_remote_copy(
            src_ref=end_ints.at[i, half_rows],
            dst_ref=end_ints.at[i, half_rows],
            send_sem=x_send.at[i],
            recv_sem=x_recv.at[i],
            device_id={"amp": 1 - column},
            device_id_type=MESH,
        )

    order = (1, 0) if proxy else (0, 1)
    pack(order[0])
    pl.semaphore_wait(barrier, n + 1 if proxy else n)
    for step, g in enumerate(order):
        if step == 1:
            pack(g)

        @pl.loop(1, n)
        def _(off):
            if g == 0 or not proxy:
                exchange(g, off)[0].start()
            else:
                d = lax.rem(me + off, n)
                to_end_run = (d == 0) | (d == n - 1)

                @pl.when(jnp.logical_not(to_end_run))
                def _():
                    exchange(1, off)[0].start()

                @pl.when(to_end_run & (jnp.clip(d, 1, n - 2) != me))
                def _():
                    to_helper(off, d).start()

        if proxy:

            @pl.when(at_end)
            def _():
                if g == 1:
                    to_helper(0, me).start()
                for i in (range(1, n - 1) if step == 1 else range(1)):
                    ints_piece(i).start()

    if proxy:

        @pl.when(is_helper)
        def _():
            for j in range(most):
                for h in range(2):
                    pool_end[h, me * most + j] = amps[1, send_tab[1, end * (most + 1) + j], h]

    for g in range(2):
        for j in range(most):
            for h in range(2):
                pools[g][h, me * most + j] = amps[g, send_tab[g, me * (most + 1) + j], h]

    for g in range(2):
        loads[g].wait()

        @pl.loop(0, BLOCKS)
        def _(b):
            columns = pl.ds(pl.multiple_of(b * block, block), block)
            high, low = split(ints[g, :, columns].T)
            ints_hi[g, columns, :] = high
            ints_lo[g, columns, :] = low

    def send_right(g, t, u, src):
        return pltpu.make_async_remote_copy(
            src_ref=src,
            dst_ref=from_left.at[g, t, piece(u)],
            send_sem=r_send.at[g, t * 2 + u],
            recv_sem=r_recv.at[g, t * 2 + u],
            device_id={"pair": lax.rem(me + 1, n)},
            device_id_type=MESH,
        )

    def send_left(g, t, u, src):
        return pltpu.make_async_remote_copy(
            src_ref=src,
            dst_ref=from_right.at[g, t, piece(u)],
            send_sem=l_send.at[g, t * 2 + u],
            recv_sem=l_recv.at[g, t * 2 + u],
            device_id={"pair": lax.rem(me - 1 + n, n)},
            device_id_type=MESH,
        )

    half = chunk // 2

    def own(t, u=None):
        if u is None:
            return pl.ds(pl.multiple_of(t * chunk, chunk), chunk)
        return pl.ds(pl.multiple_of(t * chunk + u * half, half), half)

    def piece(u):
        return pl.ds(u * half, half)

    def gather_direct(g):
        @pl.loop(1, n)
        def _(off):
            arrive, pass_on = exchange(g, off)
            arrive.wait_recv()
            pass_on.start()

        @pl.loop(1, n)
        def _(off):
            exchange(g, off)[1].wait_recv()

    def pick_rows(row, pool, hi_ref, lo_ref):
        @pl.loop(0, slots)
        def _(k):
            where = pick_tab[row, k]
            tile = jnp.concatenate([pool[0, where], pool[1, where]], axis=0)
            high, low = split(tile)
            at = pl.ds(pl.multiple_of(k * TILE, TILE), TILE)
            hi_ref[at, :] = high
            lo_ref[at, :] = low

    def product(hi_ref, lo_ref, a_hi, a_lo, at):
        dot = functools.partial(jnp.dot, preferred_element_type=jnp.float32)
        return (
            dot(hi_ref[at, :], a_lo[...])
            + dot(lo_ref[at, :], a_hi[...])
            + dot(hi_ref[at, :], a_hi[...])
        )

    def near_first(i):
        return jnp.where(me < n // 2, BLOCKS - 1 - i, i)

    def send_first(g, i):
        @pl.loop(0, per_block)
        def _(j):
            t = near_first(i) * per_block + jnp.where(me < n // 2, per_block - 1 - j, j)

            @pl.when((me == first_right[g]) & (t > me))
            def _():
                for u in range(2):
                    send_right(g, t, u, part.at[g, own(t, u)]).start()

            @pl.when((me == first_left[g]) & (t < me))
            def _():
                for u in range(2):
                    send_left(g, t, u, part.at[g, own(t, u)]).start()

    def multiply(g, b):
        at = pl.ds(pl.multiple_of(b * block, block), block)
        part[g, at, :] = product(ints_hi.at[g], ints_lo.at[g], amp_hi.at[g], amp_lo.at[g], at)

    def choose(g):
        pick_rows(g, pools[g], amp_hi.at[g], amp_lo.at[g])

    def multiply_end(i):
        ints_across(i).wait_recv()
        at = own(near_first(i))
        high, low = split(end_ints[i].T)
        end_hi[...] = high
        end_lo[...] = low
        part[1, at, :] = part[1, at, :] + product(
            end_hi, end_lo, end_amp_hi, end_amp_lo, pl.ds(0, chunk)
        )

    def take_piece(i):
        ints_piece(i).wait_recv()
        ints_across(i).start()

    if proxy:

        @pl.when(at_end)
        def _():
            gather_direct(0)
            choose(0)

            @pl.loop(0, n)
            def _(i):
                multiply(0, near_first(i))
                send_first(0, i)

            to_end().wait_recv()
            end_share().start()
            end_share().wait_recv()
            choose(1)
            multiply(1, me)

        @pl.when(is_helper)
        def _():
            @pl.loop(0, n)
            def _(home):
                @pl.when(home != me)
                def _():
                    to_helper_in = pltpu.make_async_remote_copy(
                        src_ref=packed.at[1, 0],
                        dst_ref=pool_end.at[core, pl.ds(home * most, most)],
                        send_sem=p_send.at[home],
                        recv_sem=p_recv.at[home],
                        device_id={"pair": end},
                        device_id_type=MESH,
                    )
                    to_helper_in.wait_recv()
                    end_pass(home).start()

            gather_direct(1)

            @pl.loop(0, n)
            def _(home):
                @pl.when(home != me)
                def _():
                    end_pass(home).wait_recv()

            choose(1)
            pick_rows(2, pool_end, end_amp_hi, end_amp_lo)
            take_piece(0)

            @pl.loop(0, n)
            def _(i):
                multiply(1, near_first(i))

            multiply_end(0)
            send_first(1, 0)
            gather_direct(0)
            to_end().start()
            choose(0)

            @pl.loop(0, n)
            def _(i):
                multiply(0, near_first(i))

            @pl.loop(1, n - 1)
            def _(i):
                take_piece(i)
                multiply_end(i)
                send_first(1, i)
    else:
        for g in range(2):
            gather_direct(g)
            choose(g)

            @pl.loop(0, BLOCKS)
            def _(i):
                multiply(g, near_first(i))
                send_first(g, i)

    def forward_right(g, t):
        @pl.when((t > me) & (me > first_right[g]))
        def _():
            for u in range(2):
                copy = send_right(g, t, u, from_left.at[g, t, piece(u)])
                copy.wait_recv()
                from_left[g, t, piece(u)] = from_left[g, t, piece(u)] + part[g, own(t, u), :]
                copy.start()

    def forward_left(g, t):
        @pl.when((t < me) & (me < first_left[g]))
        def _():
            for u in range(2):
                copy = send_left(g, t, u, from_right.at[g, t, piece(u)])
                copy.wait_recv()
                from_right[g, t, piece(u)] = from_right[g, t, piece(u)] + part[g, own(t, u), :]
                copy.start()

    for g in range(2):

        @pl.loop(0, n)
        def _(i):
            @pl.when(me < n // 2)
            def _():
                forward_right(g, n - 1 - i)
                forward_left(g, i)

            @pl.when(me >= n // 2)
            def _():
                forward_left(g, i)
                forward_right(g, n - 1 - i)

    for g in range(2):

        @pl.when(me > first_right[g])
        def _():
            for u in range(2):
                send_right(g, me, u, from_left.at[g, me, piece(u)]).wait_recv()
            part[g, own(me), :] = part[g, own(me), :] + from_left[g, me]

        @pl.when(me < first_left[g])
        def _():
            for u in range(2):
                send_left(g, me, u, from_right.at[g, me, piece(u)]).wait_recv()
            part[g, own(me), :] = part[g, own(me), :] + from_right[g, me]

        out[:, g, :] = residual[:, g, :] + 0.5 * part[g, own(me), :]

    for g in range(2):

        @pl.loop(1, n)
        def _(off):
            if g == 0 or not proxy:
                exchange(g, off)[0].wait_send()
                exchange(g, off)[1].wait_send()
            else:
                d = lax.rem(me + off, n)

                @pl.when(((d != 0) & (d != n - 1)) | (jnp.clip(d, 1, n - 2) != me))
                def _():
                    exchange(1, off)[0].wait_send()

                @pl.when(jnp.logical_not(at_end))
                def _():
                    exchange(1, off)[1].wait_send()

        @pl.loop(0, n)
        def _(t):
            @pl.when((t > me) & (me >= first_right[g]))
            def _():
                for u in range(2):
                    send_right(g, t, u, from_left.at[g, t, piece(u)]).wait_send()

            @pl.when((t < me) & (me <= first_left[g]))
            def _():
                for u in range(2):
                    send_left(g, t, u, from_right.at[g, t, piece(u)]).wait_send()

    if proxy:

        @pl.when(at_end)
        def _():
            to_helper(0, me).wait_send()
            end_share().wait_send()

            @pl.loop(0, n - 1)
            def _(i):
                ints_piece(i).wait_send()

        @pl.when(is_helper)
        def _():
            to_end().wait_send()

            @pl.loop(0, n)
            def _(home):
                @pl.when(home != me)
                def _():
                    end_pass(home).wait_send()

            @pl.loop(0, n - 1)
            def _(i):
                ints_across(i).wait_send()


def local(n, columns, amplitudes, integrals, tile_map, residual):
    depth, occ = amplitudes.shape[1:]
    rows = integrals.shape[2]
    slots = depth // TILE
    most = (slots + n - 1) // n
    chunk = rows // n
    proxy = n == BLOCKS and columns == 2 and chunk % 128 == 0
    smem = pl.BlockSpec(memory_space=pltpu.SMEM)
    vmem = pl.BlockSpec(memory_space=pltpu.VMEM)
    send_tab, pick_tab = pl.pallas_call(
        functools.partial(table_kernel, n, most),
        out_shape=(
            jax.ShapeDtypeStruct((2, n * (most + 1)), jnp.int32),
            jax.ShapeDtypeStruct((3, slots), jnp.int32),
        ),
        in_specs=[smem],
        out_specs=(smem, smem),
        scratch_shapes=[pltpu.SMEM((n,), jnp.int32)],
    )(tile_map)
    f32, bf16 = jnp.float32, jnp.bfloat16
    dma = pltpu.SemaphoreType.DMA
    flops = 2 * 3 * 2 * depth * rows * occ
    summed = pl.pallas_call(
        functools.partial(ladder_kernel, n, most, proxy),
        out_shape=jax.ShapeDtypeStruct((chunk, 2, occ), f32),
        in_specs=[smem, smem, vmem, pl.BlockSpec(memory_space=pl.ANY), vmem],
        out_specs=vmem,
        scratch_shapes=[
            pltpu.VMEM((2, depth, rows), f32),
            pltpu.VMEM((2, n, most, HALF, occ), f32),
            pltpu.VMEM((2, n * most, HALF, occ), f32),
            pltpu.VMEM((2, n * most, HALF, occ), f32),
            pltpu.VMEM((2, rows, depth), bf16),
            pltpu.VMEM((2, rows, depth), bf16),
            pltpu.VMEM((2, depth, occ), bf16),
            pltpu.VMEM((2, depth, occ), bf16),
            pltpu.VMEM((2, rows, occ), f32),
            pltpu.VMEM((2, n, chunk, occ), f32),
            pltpu.VMEM((2, n, chunk, occ), f32),
            pltpu.VMEM((2, n * most, HALF, occ), f32),
            pltpu.VMEM((n - 1, depth, chunk) if proxy else (1, 8, 128), f32),
            pltpu.VMEM((chunk, depth) if proxy else (16, 128), bf16),
            pltpu.VMEM((chunk, depth) if proxy else (16, 128), bf16),
            pltpu.VMEM((depth, occ), bf16),
            pltpu.VMEM((depth, occ), bf16),
            dma((2,)),
        ]
        + [dma((2, n))] * 4
        + [dma((2, 2 * n))] * 4
        + [dma((n,))] * 8
        + [dma((4,))],
        compiler_params=pltpu.CompilerParams(
            collective_id=0, has_side_effects=True, vmem_limit_bytes=56 * 1024 * 1024
        ),
        cost_estimate=pl.CostEstimate(
            flops=flops, bytes_accessed=4 * (integrals.size + amplitudes.size), transcendentals=0
        ),
    )(
        send_tab,
        pick_tab,
        amplitudes.reshape(2, slots, 2, HALF, occ),
        integrals,
        residual[0],
    )
    return summed[None]


def solution(mesh):
    placed = (
        P("groups", "pair", "amp"),
        P("groups", "pair", "rep"),
        P("groups", None),
        P("rep", "pair", "groups", "amp"),
    )
    return jax.shard_map(
        functools.partial(local, mesh.shape["pair"], mesh.shape["amp"]),
        mesh=mesh,
        in_specs=placed,
        out_specs=P("rep", "pair", "groups", "amp"),
        check_vma=False,
    )
```

```python
import functools

import jax
import jax.numpy as jnp
from jax import lax
from jax.experimental import pallas as pl
from jax.experimental.pallas import tpu as pltpu
from jax.sharding import PartitionSpec as P

TILE = 16
HALF = TILE // 2
BLOCKS = 4
MESH = pl.DeviceIdType.MESH


def table_kernel(n, most, map_ref, send_ref, pick_ref, count_ref):
    me = lax.axis_index("pair")
    slots = map_ref.shape[1] // n
    scale = ((1 << 20) + slots - 1) // slots
    low = me * slots

    for g in range(2):

        @pl.loop(0, n)
        def _(d):
            for j in range(most + 1):
                send_ref[g, d * (most + 1) + j] = 0
            found = jnp.int32(0)
            for k in range(slots):
                tile = map_ref[g, d * slots + k]
                mine = (tile >= low) & (tile < low + slots)
                send_ref[g, d * (most + 1) + found] = jnp.where(mine, tile - low, 0)
                found = found + mine.astype(jnp.int32)

        runs = [(g, me)] if g == 0 else [(1, me), (2, jnp.where(me < n // 2, 0, n - 1))]
        for row, run in runs:

            @pl.loop(0, n)
            def _(d):
                count_ref[d] = 0

            for k in range(slots):
                tile = map_ref[g, run * slots + k]
                home = lax.shift_right_logical(tile * scale, 20)
                rank = count_ref[home]
                pick_ref[row, k] = home * most + rank
                count_ref[home] = rank + 1


def split(x):
    high = x.astype(jnp.bfloat16)
    return high, (x - high.astype(jnp.float32)).astype(jnp.bfloat16)


def ladder_kernel(
    n,
    most,
    proxy,
    send_tab,
    pick_tab,
    amps,
    ints_hbm,
    residual,
    out,
    ints,
    packed,
    pool0,
    pool1,
    ints_hi,
    ints_lo,
    amp_hi,
    amp_lo,
    part,
    from_left,
    from_right,
    pool_end,
    end_ints,
    end_hi,
    end_lo,
    end_amp_hi,
    end_amp_lo,
    load_sem,
    a_send,
    a_recv,
    s_send,
    s_recv,
    r_send,
    r_recv,
    l_send,
    l_recv,
    p_send,
    p_recv,
    q_send,
    q_recv,
    i_send,
    i_recv,
    x_send,
    x_recv,
    f_sem,
):
    me = lax.axis_index("pair")
    core = lax.axis_index("rep")
    column = lax.axis_index("amp")
    end = jnp.where(me < n // 2, 0, n - 1)
    at_end = me == end
    helper = jnp.clip(end, 1, n - 2)
    is_helper = me == helper
    first_right = (0, 1 if proxy else 0)
    first_left = (n - 1, n - 2 if proxy else n - 1)
    slots = amps.shape[1]
    rows = part.shape[1]
    block = rows // BLOCKS
    chunk = rows // n
    per_block = n // BLOCKS
    pools = (pool0, pool1)

    loads = [pltpu.make_async_copy(ints_hbm.at[g], ints.at[g], load_sem.at[g]) for g in range(2)]
    for load in loads:
        load.start()

    barrier = pltpu.get_barrier_semaphore()

    @pl.loop(1, n)
    def _(off):
        pl.semaphore_signal(
            barrier, inc=1, device_id={"pair": lax.rem(me + off, n)}, device_id_type=MESH
        )

    pl.semaphore_signal(barrier, inc=1, device_id={"rep": 1 - core}, device_id_type=MESH)
    if proxy:
        pl.semaphore_signal(barrier, inc=1, device_id={"amp": 1 - column}, device_id_type=MESH)

    def pack(g):
        @pl.loop(0 if proxy and g == 1 else 1, n)
        def _(off):
            d = lax.rem(me + off, n)
            for j in range(most):
                packed[g, off, j] = amps[g, send_tab[g, d * (most + 1) + j], core]

    def exchange(g, off):
        source = lax.rem(me - off + n, n)
        target = lax.rem(me + off, n)
        return (
            pltpu.make_async_remote_copy(
                src_ref=packed.at[g, off],
                dst_ref=pools[g].at[core, pl.ds(me * most, most)],
                send_sem=a_send.at[g, off],
                recv_sem=a_recv.at[g, off],
                device_id={"pair": target},
                device_id_type=MESH,
            ),
            pltpu.make_async_remote_copy(
                src_ref=pools[g].at[core, pl.ds(source * most, most)],
                dst_ref=pools[g].at[core, pl.ds(source * most, most)],
                send_sem=s_send.at[g, off],
                recv_sem=s_recv.at[g, off],
                device_id={"rep": 1 - core},
                device_id_type=MESH,
            ),
        )

    def to_helper(off, d):
        return pltpu.make_async_remote_copy(
            src_ref=packed.at[1, off],
            dst_ref=pool_end.at[core, pl.ds(me * most, most)],
            send_sem=a_send.at[1, off],
            recv_sem=p_recv.at[me],
            device_id={"pair": jnp.clip(d, 1, n - 2)},
            device_id_type=MESH,
        )

    def end_pass(home):
        rows_at = (core, pl.ds(home * most, most))
        return pltpu.make_async_remote_copy(
            src_ref=pool_end.at[rows_at],
            dst_ref=pool_end.at[rows_at],
            send_sem=q_send.at[home],
            recv_sem=q_recv.at[home],
            device_id={"rep": 1 - core},
            device_id_type=MESH,
        )

    others = (core, pl.ds(jnp.where(end == 0, most, 0), (n - 1) * most))

    def to_end():
        return pltpu.make_async_remote_copy(
            src_ref=pool_end.at[others],
            dst_ref=pool1.at[others],
            send_sem=f_sem.at[0],
            recv_sem=f_sem.at[1],
            device_id={"pair": end},
            device_id_type=MESH,
        )

    def end_share():
        return pltpu.make_async_remote_copy(
            src_ref=pool1.at[others],
            dst_ref=pool1.at[others],
            send_sem=f_sem.at[2],
            recv_sem=f_sem.at[3],
            device_id={"rep": 1 - core},
            device_id_type=MESH,
        )

    half_rows = pl.ds(
        pl.multiple_of(column * (slots * HALF), HALF), slots * HALF
    )

    def ints_piece(i):
        b = jnp.where(end == 0, n - 1 - i, i)
        return pltpu.make_async_remote_copy(
            src_ref=ints_hbm.at[
                1, half_rows, pl.ds(pl.multiple_of(b * chunk, chunk), chunk)
            ],
            dst_ref=end_ints.at[i, half_rows],
            send_sem=i_send.at[i],
            recv_sem=i_recv.at[i],
            device_id={"pair": helper},
            device_id_type=MESH,
        )

    def ints_across(i):
        return pltpu.make_async_remote_copy(
            src_ref=end_ints.at[i, half_rows],
            dst_ref=end_ints.at[i, half_rows],
            send_sem=x_send.at[i],
            recv_sem=x_recv.at[i],
            device_id={"amp": 1 - column},
            device_id_type=MESH,
        )

    order = (1, 0) if proxy else (0, 1)
    pack(order[0])
    pl.semaphore_wait(barrier, n + 1 if proxy else n)
    for step, g in enumerate(order):
        if step == 1:
            pack(g)

        @pl.loop(1, n)
        def _(off):
            if g == 0 or not proxy:
                exchange(g, off)[0].start()
            else:
                d = lax.rem(me + off, n)
                to_end_run = (d == 0) | (d == n - 1)

                @pl.when(jnp.logical_not(to_end_run))
                def _():
                    exchange(1, off)[0].start()

                @pl.when(to_end_run & (jnp.clip(d, 1, n - 2) != me))
                def _():
                    to_helper(off, d).start()

        if proxy:

            @pl.when(at_end)
            def _():
                if g == 1:
                    to_helper(0, me).start()
                for i in (range(1, n - 1) if step == 1 else range(1)):
                    ints_piece(i).start()

    if proxy:

        @pl.when(is_helper)
        def _():
            for j in range(most):
                for h in range(2):
                    pool_end[h, me * most + j] = amps[1, send_tab[1, end * (most + 1) + j], h]

    for g in range(2):
        for j in range(most):
            for h in range(2):
                pools[g][h, me * most + j] = amps[g, send_tab[g, me * (most + 1) + j], h]

    for g in range(2):
        loads[g].wait()

        @pl.loop(0, BLOCKS)
        def _(b):
            columns = pl.ds(pl.multiple_of(b * block, block), block)
            high, low = split(ints[g, :, columns].T)
            ints_hi[g, columns, :] = high
            ints_lo[g, columns, :] = low

    def send_right(g, t, u, src):
        return pltpu.make_async_remote_copy(
            src_ref=src,
            dst_ref=from_left.at[g, t, piece(u)],
            send_sem=r_send.at[g, t * 2 + u],
            recv_sem=r_recv.at[g, t * 2 + u],
            device_id={"pair": lax.rem(me + 1, n)},
            device_id_type=MESH,
        )

    def send_left(g, t, u, src):
        return pltpu.make_async_remote_copy(
            src_ref=src,
            dst_ref=from_right.at[g, t, piece(u)],
            send_sem=l_send.at[g, t * 2 + u],
            recv_sem=l_recv.at[g, t * 2 + u],
            device_id={"pair": lax.rem(me - 1 + n, n)},
            device_id_type=MESH,
        )

    half = chunk // 2

    def own(t, u=None):
        if u is None:
            return pl.ds(pl.multiple_of(t * chunk, chunk), chunk)
        return pl.ds(pl.multiple_of(t * chunk + u * half, half), half)

    def piece(u):
        return pl.ds(u * half, half)

    def gather_direct(g):
        @pl.loop(1, n)
        def _(off):
            arrive, pass_on = exchange(g, off)
            arrive.wait_recv()
            pass_on.start()

        @pl.loop(1, n)
        def _(off):
            exchange(g, off)[1].wait_recv()

    def pick_rows(row, pool, hi_ref, lo_ref):
        @pl.loop(0, slots)
        def _(k):
            where = pick_tab[row, k]
            tile = jnp.concatenate([pool[0, where], pool[1, where]], axis=0)
            high, low = split(tile)
            at = pl.ds(pl.multiple_of(k * TILE, TILE), TILE)
            hi_ref[at, :] = high
            lo_ref[at, :] = low

    def product(hi_ref, lo_ref, a_hi, a_lo, at):
        dot = functools.partial(jnp.dot, preferred_element_type=jnp.float32)
        return (
            dot(hi_ref[at, :], a_lo[...])
            + dot(lo_ref[at, :], a_hi[...])
            + dot(hi_ref[at, :], a_hi[...])
        )

    def near_first(i):
        return jnp.where(me < n // 2, BLOCKS - 1 - i, i)

    def send_first(g, i):
        @pl.loop(0, per_block)
        def _(j):
            t = near_first(i) * per_block + jnp.where(me < n // 2, per_block - 1 - j, j)

            @pl.when((me == first_right[g]) & (t > me))
            def _():
                for u in range(2):
                    send_right(g, t, u, part.at[g, own(t, u)]).start()

            @pl.when((me == first_left[g]) & (t < me))
            def _():
                for u in range(2):
                    send_left(g, t, u, part.at[g, own(t, u)]).start()

    def multiply(g, b):
        at = pl.ds(pl.multiple_of(b * block, block), block)
        part[g, at, :] = product(ints_hi.at[g], ints_lo.at[g], amp_hi.at[g], amp_lo.at[g], at)

    def choose(g):
        pick_rows(g, pools[g], amp_hi.at[g], amp_lo.at[g])

    def multiply_end(i):
        ints_across(i).wait_recv()
        at = own(near_first(i))
        high, low = split(end_ints[i].T)
        end_hi[...] = high
        end_lo[...] = low
        part[1, at, :] = part[1, at, :] + product(
            end_hi, end_lo, end_amp_hi, end_amp_lo, pl.ds(0, chunk)
        )

    def take_piece(i):
        ints_piece(i).wait_recv()
        ints_across(i).start()

    if proxy:

        @pl.when(at_end)
        def _():
            gather_direct(0)
            choose(0)

            @pl.loop(0, n)
            def _(i):
                multiply(0, near_first(i))
                send_first(0, i)

            to_end().wait_recv()
            end_share().start()
            end_share().wait_recv()
            choose(1)
            multiply(1, me)

        @pl.when(is_helper)
        def _():
            @pl.loop(0, n)
            def _(home):
                @pl.when(home != me)
                def _():
                    to_helper_in = pltpu.make_async_remote_copy(
                        src_ref=packed.at[1, 0],
                        dst_ref=pool_end.at[core, pl.ds(home * most, most)],
                        send_sem=p_send.at[home],
                        recv_sem=p_recv.at[home],
                        device_id={"pair": end},
                        device_id_type=MESH,
                    )
                    to_helper_in.wait_recv()
                    end_pass(home).start()

            gather_direct(1)

            @pl.loop(0, n)
            def _(home):
                @pl.when(home != me)
                def _():
                    end_pass(home).wait_recv()

            take_piece(0)
            choose(1)
            pick_rows(2, pool_end, end_amp_hi, end_amp_lo)
            multiply(1, near_first(0))
            multiply_end(0)
            send_first(1, 0)

            @pl.loop(1, n)
            def _(i):
                multiply(1, near_first(i))

            gather_direct(0)
            to_end().start()
            choose(0)

            @pl.loop(0, n)
            def _(i):
                multiply(0, near_first(i))

            @pl.loop(1, n - 1)
            def _(i):
                take_piece(i)
                multiply_end(i)
                send_first(1, i)
    else:
        for g in range(2):
            gather_direct(g)
            choose(g)

            @pl.loop(0, BLOCKS)
            def _(i):
                multiply(g, near_first(i))
                send_first(g, i)

    def forward_right(g, t):
        @pl.when((t > me) & (me > first_right[g]))
        def _():
            for u in range(2):
                copy = send_right(g, t, u, from_left.at[g, t, piece(u)])
                copy.wait_recv()
                from_left[g, t, piece(u)] = from_left[g, t, piece(u)] + part[g, own(t, u), :]
                copy.start()

    def forward_left(g, t):
        @pl.when((t < me) & (me < first_left[g]))
        def _():
            for u in range(2):
                copy = send_left(g, t, u, from_right.at[g, t, piece(u)])
                copy.wait_recv()
                from_right[g, t, piece(u)] = from_right[g, t, piece(u)] + part[g, own(t, u), :]
                copy.start()

    for g in range(2):

        @pl.loop(0, n)
        def _(i):
            @pl.when(me < n // 2)
            def _():
                forward_right(g, n - 1 - i)
                forward_left(g, i)

            @pl.when(me >= n // 2)
            def _():
                forward_left(g, i)
                forward_right(g, n - 1 - i)

    for g in range(2):

        @pl.when(me > first_right[g])
        def _():
            for u in range(2):
                send_right(g, me, u, from_left.at[g, me, piece(u)]).wait_recv()
            part[g, own(me), :] = part[g, own(me), :] + from_left[g, me]

        @pl.when(me < first_left[g])
        def _():
            for u in range(2):
                send_left(g, me, u, from_right.at[g, me, piece(u)]).wait_recv()
            part[g, own(me), :] = part[g, own(me), :] + from_right[g, me]

        out[:, g, :] = residual[:, g, :] + 0.5 * part[g, own(me), :]

    for g in range(2):

        @pl.loop(1, n)
        def _(off):
            if g == 0 or not proxy:
                exchange(g, off)[0].wait_send()
                exchange(g, off)[1].wait_send()
            else:
                d = lax.rem(me + off, n)

                @pl.when(((d != 0) & (d != n - 1)) | (jnp.clip(d, 1, n - 2) != me))
                def _():
                    exchange(1, off)[0].wait_send()

                @pl.when(jnp.logical_not(at_end))
                def _():
                    exchange(1, off)[1].wait_send()

        @pl.loop(0, n)
        def _(t):
            @pl.when((t > me) & (me >= first_right[g]))
            def _():
                for u in range(2):
                    send_right(g, t, u, from_left.at[g, t, piece(u)]).wait_send()

            @pl.when((t < me) & (me <= first_left[g]))
            def _():
                for u in range(2):
                    send_left(g, t, u, from_right.at[g, t, piece(u)]).wait_send()

    if proxy:

        @pl.when(at_end)
        def _():
            to_helper(0, me).wait_send()
            end_share().wait_send()

            @pl.loop(0, n - 1)
            def _(i):
                ints_piece(i).wait_send()

        @pl.when(is_helper)
        def _():
            to_end().wait_send()

            @pl.loop(0, n)
            def _(home):
                @pl.when(home != me)
                def _():
                    end_pass(home).wait_send()

            @pl.loop(0, n - 1)
            def _(i):
                ints_across(i).wait_send()


def local(n, columns, amplitudes, integrals, tile_map, residual):
    depth, occ = amplitudes.shape[1:]
    rows = integrals.shape[2]
    slots = depth // TILE
    most = (slots + n - 1) // n
    chunk = rows // n
    proxy = n == BLOCKS and columns == 2 and chunk % 128 == 0
    smem = pl.BlockSpec(memory_space=pltpu.SMEM)
    vmem = pl.BlockSpec(memory_space=pltpu.VMEM)
    send_tab, pick_tab = pl.pallas_call(
        functools.partial(table_kernel, n, most),
        out_shape=(
            jax.ShapeDtypeStruct((2, n * (most + 1)), jnp.int32),
            jax.ShapeDtypeStruct((3, slots), jnp.int32),
        ),
        in_specs=[smem],
        out_specs=(smem, smem),
        scratch_shapes=[pltpu.SMEM((n,), jnp.int32)],
    )(tile_map)
    f32, bf16 = jnp.float32, jnp.bfloat16
    dma = pltpu.SemaphoreType.DMA
    flops = 2 * 3 * 2 * depth * rows * occ
    summed = pl.pallas_call(
        functools.partial(ladder_kernel, n, most, proxy),
        out_shape=jax.ShapeDtypeStruct((chunk, 2, occ), f32),
        in_specs=[smem, smem, vmem, pl.BlockSpec(memory_space=pl.ANY), vmem],
        out_specs=vmem,
        scratch_shapes=[
            pltpu.VMEM((2, depth, rows), f32),
            pltpu.VMEM((2, n, most, HALF, occ), f32),
            pltpu.VMEM((2, n * most, HALF, occ), f32),
            pltpu.VMEM((2, n * most, HALF, occ), f32),
            pltpu.VMEM((2, rows, depth), bf16),
            pltpu.VMEM((2, rows, depth), bf16),
            pltpu.VMEM((2, depth, occ), bf16),
            pltpu.VMEM((2, depth, occ), bf16),
            pltpu.VMEM((2, rows, occ), f32),
            pltpu.VMEM((2, n, chunk, occ), f32),
            pltpu.VMEM((2, n, chunk, occ), f32),
            pltpu.VMEM((2, n * most, HALF, occ), f32),
            pltpu.VMEM((n - 1, depth, chunk) if proxy else (1, 8, 128), f32),
            pltpu.VMEM((chunk, depth) if proxy else (16, 128), bf16),
            pltpu.VMEM((chunk, depth) if proxy else (16, 128), bf16),
            pltpu.VMEM((depth, occ), bf16),
            pltpu.VMEM((depth, occ), bf16),
            dma((2,)),
        ]
        + [dma((2, n))] * 4
        + [dma((2, 2 * n))] * 4
        + [dma((n,))] * 8
        + [dma((4,))],
        compiler_params=pltpu.CompilerParams(
            collective_id=0, has_side_effects=True, vmem_limit_bytes=56 * 1024 * 1024
        ),
        cost_estimate=pl.CostEstimate(
            flops=flops, bytes_accessed=4 * (integrals.size + amplitudes.size), transcendentals=0
        ),
    )(
        send_tab,
        pick_tab,
        amplitudes.reshape(2, slots, 2, HALF, occ),
        integrals,
        residual[0],
    )
    return summed[None]


def solution(mesh):
    placed = (
        P("groups", "pair", "amp"),
        P("groups", "pair", "rep"),
        P("groups", None),
        P("rep", "pair", "groups", "amp"),
    )
    return jax.shard_map(
        functools.partial(local, mesh.shape["pair"], mesh.shape["amp"]),
        mesh=mesh,
        in_specs=placed,
        out_specs=P("rep", "pair", "groups", "amp"),
        check_vma=False,
    )
```
